256 devices in a mesh: row: 32 (over y, x, core), col: 8 (over z).
Axes of the slice: x: 4, y: 4, z: 8, core: 2. Of those that a mesh axis runs over, the one named last changes fastest.
Arguments:
- queries: bfloat16 [16384, 3072], P('row', 'col'), may hold values from -6 to 6
- keys_in: bfloat16 [16384, 3072], P('row', 'col'), may hold values from -6 to 6
- values_in: bfloat16 [16384, 3072], P('row', 'col'), may hold values from -6 to 6
- query_gain: float32 [3072], P('col'), may hold values from 0.1 to 1.9
- key_gain: float32 [3072], P('col'), may hold values from 0.1 to 1.9
- out_weight: bfloat16 [3072, 6144], P('row', 'col'), may hold values from -0.109375 to 0.109375
- cotangent: bfloat16 [16384, 6144], P('row', 'col'), may hold values from -6 to 6
Outputs:
- output: bfloat16 [16384, 6144], P('row', 'col')
- grad_queries: bfloat16 [16384, 3072], P('row', 'col')
- grad_keys: bfloat16 [16384, 3072], P('row', 'col')
- grad_values: bfloat16 [16384, 3072], P('row', 'col')
- grad_weight: bfloat16 [3072, 6144], P('row', 'col')
The draws below stay inside these ranges and needn't reach their ends.
All inputs are finite; a program needn't handle non-finite values.
Results may differ from the reference program's by a relative error of at most 0.0087.
Values may be sent and summed in bfloat16 or wider, within the bound.
A program may use at most 128 MiB of HBM per device.

```python
import jax
import jax.numpy as jnp
from jax import lax

D = 6144
HEADS = 24
HEAD_DIM = 128
PATCHES = 256
E = 3072
TOKENS = 16384
IMAGES = 64


def block_scale(key, extent, split, least, high):
    factor_of, own = 1.0, jax.random.fold_in(key, 6)
    for axis_at, shards_of in split:
        heights = jnp.exp(jax.random.uniform(jax.random.fold_in(own, axis_at), (shards_of,), jnp.float32, least / len(split), high / len(split)))
        factor_of = factor_of * jnp.repeat(heights, extent[axis_at] // shards_of).reshape([-1 if axis == axis_at else 1 for axis in range(len(extent))])
    return factor_of


def normal_values(rng, dims, width, bound, split=(), dtype=jnp.bfloat16):
    drawn = width * jax.random.normal(rng, dims, jnp.float32)
    if split:
        drawn = drawn * block_scale(rng, dims, split, -0.22, 0.18)
    return jnp.clip(drawn, -bound, bound).astype(dtype)


def setup_inputs(seed: int = 0) -> dict:
    key_of = jax.random.split(jax.random.key(seed), 8)
    queries = normal_values(key_of[0], (TOKENS, E), 1.0, 6.0, ((0, 32), (1, 8)))
    keys_in = normal_values(key_of[1], (TOKENS, E), 1.0, 6.0, ((0, 32), (1, 8)))
    values_in = normal_values(key_of[2], (TOKENS, E), 1.0, 6.0, ((0, 32), (1, 8)))
    query_gain = jnp.clip(1.0 + 0.18 * jax.random.normal(key_of[3], (E,), jnp.float32), 0.1, 1.9)
    key_gain = jnp.clip(1.0 + 0.18 * jax.random.normal(key_of[4], (E,), jnp.float32), 0.1, 1.9)
    out_weight = normal_values(key_of[5], (E, D), E ** -0.5, 0.109375, ((0, 32), (1, 8)))
    cotangent = normal_values(key_of[6], (TOKENS, D), 1.0, 6.0, ((0, 32), (1, 8)))
    return {"queries": queries, "keys_in": keys_in, "values_in": values_in, "query_gain": query_gain, "key_gain": key_gain, "out_weight": out_weight, "cotangent": cotangent}


epsilon = 1e-06

def head_norm(inside, scaling):
    average = lax.optimization_barrier(jnp.mean(inside, axis=-1, keepdims=True))
    centred = inside - average
    spread = lax.optimization_barrier(jnp.mean(centred * centred, axis=-1, keepdims=True))
    return centred * lax.rsqrt(spread + epsilon) * scaling

def product(pattern, first_op, second_op):
    first_op, second_op = lax.optimization_barrier((first_op, second_op))
    return jnp.einsum(pattern, first_op.astype(jnp.float32), second_op.astype(jnp.float32))

def attend(queries, keys_in, values_in, query_gains, key_gains):
    score_scale = queries.shape[-1] ** (-0.5)
    query_norm = head_norm(queries.astype(jnp.float32), query_gains).astype(jnp.bfloat16)
    key_norm = head_norm(keys_in.astype(jnp.float32), key_gains).astype(jnp.bfloat16)
    scores = product('nqhd,nkhd->nhqk', query_norm, key_norm) * score_scale
    weights = jnp.exp(scores)
    probabilities = weights / lax.optimization_barrier(jnp.sum(weights, axis=-1, keepdims=True))
    prob_low = probabilities.astype(jnp.bfloat16)
    attended = product('nhqk,nkhd->nqhd', prob_low, values_in).astype(jnp.bfloat16)
    return (query_norm, key_norm, probabilities, prob_low, attended)

def attend_back(queries, keys_in, values_in, query_gains, key_gains, query_norm, key_norm, probabilities, prob_low, grad_attended):
    score_scale = queries.shape[-1] ** (-0.5)
    grad_probs = product('nqhd,nkhd->nhqk', grad_attended, values_in)
    inner_sum = lax.optimization_barrier(jnp.sum(probabilities * grad_probs, axis=-1, keepdims=True))
    grad_scores = (probabilities * (grad_probs - inner_sum) * score_scale).astype(jnp.bfloat16)
    grad_values = product('nhqk,nqhd->nkhd', prob_low, grad_attended).astype(jnp.bfloat16)
    grad_qnorm = product('nhqk,nkhd->nqhd', grad_scores, key_norm)
    grad_knorm = product('nhqk,nqhd->nkhd', grad_scores, query_norm)
    unused, query_pull = jax.vjp(lambda inside: head_norm(inside, query_gains), queries.astype(jnp.float32))
    unused, key_pull = jax.vjp(lambda inside: head_norm(inside, key_gains), keys_in.astype(jnp.float32))
    grad_queries = query_pull(grad_qnorm)[0].astype(jnp.bfloat16)
    grad_keys = key_pull(grad_knorm)[0].astype(jnp.bfloat16)
    return (grad_queries, grad_keys, grad_values)

def reference(queries, keys_in, values_in, query_gain, key_gain, out_weight, cotangent):
    image_shape = (IMAGES, PATCHES, HEADS, HEAD_DIM)
    query_blocks = queries.reshape(image_shape)
    key_blocks = keys_in.reshape(image_shape)
    value_blocks = values_in.reshape(image_shape)
    query_gains = query_gain.reshape(HEADS, HEAD_DIM)
    key_gains = key_gain.reshape(HEADS, HEAD_DIM)

    def forward_one(operands):
        query_one, key_one, value_one = operands
        return attend(query_one[None], key_one[None], value_one[None], query_gains, key_gains)[4][0]
    attended = lax.map(forward_one, (query_blocks, key_blocks, value_blocks)).reshape(TOKENS, HEADS * HEAD_DIM)
    output = jnp.dot(attended, out_weight, preferred_element_type=jnp.float32).astype(jnp.bfloat16)
    grad_attended = lax.dot_general(cotangent, out_weight, (((1,), (1,)), ((), ())), preferred_element_type=jnp.float32).astype(jnp.bfloat16)
    grad_weight = lax.dot_general(attended, cotangent, (((0,), (0,)), ((), ())), preferred_element_type=jnp.float32).astype(jnp.bfloat16)
    grad_blocks = grad_attended.reshape(image_shape)

    def backward_one(operands):
        query_one, key_one, value_one, grad_one = operands
        stored = attend(query_one[None], key_one[None], value_one[None], query_gains, key_gains)
        gradients = attend_back(query_one[None], key_one[None], value_one[None], query_gains, key_gains, stored[0], stored[1], stored[2], stored[3], grad_one[None])
        return (gradients[0][0], gradients[1][0], gradients[2][0])
    grad_q, grad_k, grad_v = lax.map(backward_one, (query_blocks, key_blocks, value_blocks, grad_blocks))
    flat_shape = (TOKENS, HEADS * HEAD_DIM)
    return (output, grad_q.reshape(flat_shape), grad_k.reshape(flat_shape), grad_v.reshape(flat_shape), grad_weight)
```

```python
import jax
import jax.numpy as jnp
from jax import lax
from jax.experimental import pallas as pl
from jax.experimental.pallas import tpu as pltpu
from jax.sharding import PartitionSpec as P

HEAD_DIM = 128
PATCHES = 256
HEADS_HERE = 3
NX, NY, NZ = 4, 4, 8
SHARD_ROWS = 96
HALF_ROWS = 48
HALF_COLS = 384
EPSILON = 1e-06
MESH = pl.DeviceIdType.MESH
BF16 = jnp.bfloat16
F32 = jnp.float32


def dot_nn(a, b):
    return jnp.dot(a, b, preferred_element_type=F32)


def dot_nt(a, b):
    return lax.dot_general(a, b, (((1,), (1,)), ((), ())), preferred_element_type=F32)


def dot_tn(a, b):
    return lax.dot_general(a, b, (((0,), (0,)), ((), ())), preferred_element_type=F32)


def block_kernel(
    q_ref, k_ref, v_ref, qg_ref, kg_ref, w_ref, ct_ref,
    out_ref, gq_ref, gk_ref, gv_ref, gw_ref,
    wall, aall, prob, plow, qhat, khat, qrs, krs, qn, kn,
    gsend, grecv, gwb, sib, s1, r1, s2, r2, c1,
    w1_send, w1_recv, w2_send, w2_recv, ws0_send, ws0_recv, ws1_send, ws1_recv, ws2_send, ws2_recv,
    a_send, a_recv, g_send, g_recv, sib_send, sib_recv, p1_send, p1_recv, p2_send, p2_recv,
):
    row = lax.axis_index("row")
    z = lax.axis_index("col")
    core = lax.rem(row, 2)
    x = lax.rem(lax.div(row, 2), NX)
    y = lax.div(row, 2 * NX)
    scale = HEAD_DIM ** (-0.5)

    def device(yy, xx, cc, zz):
        return ((yy * NX + xx) * 2 + cc, zz)

    def x_turn(j):
        return device(y, lax.rem(x + 1 + 2 * j, NX), core, z)

    def y_turn(j):
        return device(lax.rem(y + 1 + 2 * j, NY), x, core, z)

    def z_turn(image):
        return (row, lax.rem(z + 1 + 6 * image, NZ))

    sibling = device(y, x, 1 - core, z)

    barrier = pltpu.get_barrier_semaphore()
    for peer in (x_turn(0), x_turn(1), y_turn(0), y_turn(1), z_turn(0), z_turn(1), sibling):
        pl.semaphore_signal(barrier, inc=1, device_id=peer, device_id_type=MESH)
    pl.semaphore_wait(barrier, 7)

    def remote(src, dst, send, recv, peer):
        return pltpu.make_async_remote_copy(
            src_ref=src, dst_ref=dst, send_sem=send, recv_sem=recv, device_id=peer, device_id_type=MESH
        )

    def behind(pos, steps, j):
        return lax.rem(pos + (4 - steps if j == 0 else steps), 4)

    def w1_ref(i, j, steps):
        if i == 0:
            return wall.at[j, y, behind(x, steps, j), core, i]
        return wall.at[j, behind(y, steps, j), x, core, i]

    def w2_ref(i, j, steps):
        if i == 0:
            return wall.at[j, behind(y, steps, j), :, core, i]
        return wall.at[j, :, behind(x, steps, j), core, i]

    def w1_copy(i, j, s):
        ref = w1_ref(i, j, s)
        return remote(ref, ref, w1_send.at[i, j, s], w1_recv.at[i, j, s], x_turn(j) if i == 0 else y_turn(j))

    def w2_copy(i, j, s):
        ref = w2_ref(i, j, s)
        return remote(ref, ref, w2_send.at[i, j, s], w2_recv.at[i, j, s], y_turn(j) if i == 0 else x_turn(j))

    def ws0_copy():
        ref = wall.at[:, y, x, core]
        return remote(ref, ref, ws0_send, ws0_recv, sibling)

    def ws1_copy(i, j, s):
        ref = w1_ref(i, j, s + 1)
        return remote(ref, ref, ws1_send.at[i, j, s], ws1_recv.at[i, j, s], sibling)

    def ws2_copy(i, j, s):
        ref = w2_ref(i, j, s + 1)
        return remote(ref, ref, ws2_send.at[i, j, s], ws2_recv.at[i, j, s], sibling)

    quarters = [(i, j) for i in range(2) for j in range(2)]

    def weight_step(t):
        for i, j in quarters:
            if t < 3:
                w1_copy(i, j, t).wait_recv()
                if t < 2:
                    w1_copy(i, j, t + 1).start()
                else:
                    w2_copy(i, j, 0).start()
                ws1_copy(i, j, t).start()
            else:
                w2_copy(i, j, t - 3).wait_recv()
                if t < 5:
                    w2_copy(i, j, t - 2).start()
                ws2_copy(i, j, t - 3).start()

    def weight_wait():
        ws0_copy().wait_recv()
        for i, j in quarters:
            for s in range(3):
                ws1_copy(i, j, s).wait_recv()
                ws2_copy(i, j, s).wait_recv()

    def weight_sent():
        ws0_copy().wait_send()
        for i, j in quarters:
            for s in range(3):
                w1_copy(i, j, s).wait_send()
                w2_copy(i, j, s).wait_send()
                ws1_copy(i, j, s).wait_send()
                ws2_copy(i, j, s).wait_send()

    def a_copy(image, s, h):
        origin = lax.rem(z + (NZ - s if image == 0 else s), NZ)
        ref = aall.at[origin * HEADS_HERE + h, pl.ds(image * PATCHES, PATCHES)]
        return remote(ref, ref, a_send.at[image, s, h], a_recv.at[image, s, h], z_turn(image))

    def a_pass(s, h):
        for image in range(2):
            a_copy(image, s - 1, h).wait_recv()
            a_copy(image, s, h).start()

    def head_slice(image, h):
        return (pl.ds(image * PATCHES, PATCHES), pl.ds(pl.multiple_of(h * HEAD_DIM, HEAD_DIM), HEAD_DIM))

    def norm_forward(image, h, source, gain, hat, spread_ref, normed):
        inside = source[head_slice(image, h)].astype(F32)
        centred = inside - jnp.mean(inside, axis=-1, keepdims=True)
        spread = jnp.mean(centred * centred, axis=-1, keepdims=True)
        factor = lax.rsqrt(spread + EPSILON)
        unit = centred * factor
        hat[image, h] = unit
        spread_ref[image, h] = jnp.broadcast_to(factor, unit.shape)
        value = (unit * gain[h]).astype(BF16)
        normed[image, h] = value
        return value

    def forward(image, h):
        q_norm = norm_forward(image, h, q_ref, qg_ref, qhat, qrs, qn)
        k_norm = norm_forward(image, h, k_ref, kg_ref, khat, krs, kn)
        weights = jnp.exp(dot_nt(q_norm, k_norm) * scale)
        probabilities = weights * (1.0 / jnp.sum(weights, axis=-1, keepdims=True))
        low = probabilities.astype(BF16)
        prob[image, h] = probabilities
        plow[image, h] = low
        attended = dot_nn(low, v_ref[head_slice(image, h)]).astype(BF16)
        aall[z * HEADS_HERE + h, pl.ds(image * PATCHES, PATCHES)] = attended

    def norm_backward(grad, image, h, gain, hat, spread_ref):
        scaled = grad * gain[h]
        unit = hat[image, h]
        first = jnp.mean(scaled, axis=-1, keepdims=True)
        second = jnp.mean(scaled * unit, axis=-1, keepdims=True)
        return (spread_ref[image, h] * (scaled - first - unit * second)).astype(BF16)

    def backward(image, h, grad_attended):
        place = head_slice(image, h)
        probabilities = prob[image, h]
        gv_ref[place] = dot_tn(plow[image, h], grad_attended).astype(BF16)
        grad_probs = dot_nt(grad_attended, v_ref[place])
        inner = jnp.sum(probabilities * grad_probs, axis=-1, keepdims=True)
        grad_scores = (probabilities * (grad_probs - inner) * scale).astype(BF16)
        grad_q = dot_nn(grad_scores, kn[image, h])
        grad_k = dot_tn(grad_scores, qn[image, h])
        gq_ref[place] = norm_backward(grad_q, image, h, qg_ref, qhat, qrs)
        gk_ref[place] = norm_backward(grad_k, image, h, kg_ref, khat, krs)

    def weight_rows(j, o):
        piece = wall[j, lax.div(o, 2), pl.ds(2 * lax.rem(o, 2), 2)]
        return piece.reshape(HEADS_HERE * HEAD_DIM, HALF_COLS)

    def g_copy(image, s, h):
        return remote(
            gsend.at[image, s, h], grecv.at[image, s, h], g_send.at[image, s, h], g_recv.at[image, s, h], z_turn(image)
        )

    def g_term(image, s):
        owner = lax.rem(z + (2 * NZ - 1 - s if image == 0 else 1 + s), NZ)
        rows = pl.ds(image * PATCHES, PATCHES)
        return dot_nt(ct_ref[rows, :HALF_COLS], weight_rows(0, owner)) + dot_nt(
            ct_ref[rows, HALF_COLS:], weight_rows(1, owner)
        )

    def head_columns(value, h):
        return value[:, h * HEAD_DIM : (h + 1) * HEAD_DIM]

    def g_first():
        for image in range(2):
            term = g_term(image, 0)
            for h in range(HEADS_HERE):
                gsend[image, 0, h] = head_columns(term, h).astype(BF16)
                g_copy(image, 0, h).start()

    def g_step(s):
        terms = [g_term(image, s) for image in range(2)]
        for h in range(HEADS_HERE):
            for image in range(2):
                g_copy(image, s - 1, h).wait_recv()
                total = head_columns(terms[image], h) + grecv[image, s - 1, h].astype(F32)
                gsend[image, s, h] = total.astype(BF16)
                g_copy(image, s, h).start()

    def gw_copy(index, o):
        place = pl.ds(2 * lax.rem(o, 2), 2)
        return remote(
            gwb.at[1 - core, lax.div(o, 2), place],
            sib.at[lax.div(o, 2), place],
            sib_send.at[index],
            sib_recv.at[index],
            sibling,
        )

    def gw_block(index, o):
        panel = jnp.concatenate([aall[o * HEADS_HERE + h] for h in range(HEADS_HERE)], axis=1)
        for j in range(2):
            value = dot_tn(panel, ct_ref[:, j * HALF_COLS : (j + 1) * HALF_COLS]).astype(BF16)
            for xx in range(2):
                for cc in range(2):
                    for i in range(2):
                        at = (xx * 4 + cc * 2 + i) * HALF_ROWS
                        gwb[cc, lax.div(o, 2), 2 * lax.rem(o, 2) + xx, i, j] = value[at : at + HALF_ROWS]
        gw_copy(index, o).start()

    def gw_owner(index):
        return lax.rem(z + index, NZ)

    def chip_sum(i, j, d):
        if i == 0:
            return gwb[core, :, d, i, j].astype(F32) + sib[:, d, i, j].astype(F32)
        return gwb[core, d, :, i, j].astype(F32) + sib[d, :, i, j].astype(F32)

    def p1_copy(i, j, s):
        peer = x_turn(j) if i == 0 else y_turn(j)
        return remote(s1.at[i, j, s], r1.at[i, j, s], p1_send.at[i, j, s], p1_recv.at[i, j, s], peer)

    def p2_copy(i, j, s):
        peer = y_turn(j) if i == 0 else x_turn(j)
        return remote(s2.at[i, j, s], r2.at[i, j, s], p2_send.at[i, j, s], p2_recv.at[i, j, s], peer)

    def scatter_step(t):
        for i, j in quarters:
            first, second = (x, y) if i == 0 else (y, x)
            if t <= 3:
                total = chip_sum(i, j, behind(first, (1 + t) % 4, j))
                if t > 0:
                    p1_copy(i, j, t - 1).wait_recv()
                    total = total + r1[i, j, t - 1].astype(F32)
                if t < 3:
                    s1[i, j, t] = total.astype(BF16)
                    p1_copy(i, j, t).start()
                else:
                    c1[i, j] = total
                    s2[i, j, 0] = c1[i, j, behind(second, 1, j)].astype(BF16)
                    p2_copy(i, j, 0).start()
            else:
                s = t - 4
                p2_copy(i, j, s).wait_recv()
                total = c1[i, j, behind(second, (2 + s) % 4, j)] + r2[i, j, s].astype(F32)
                if s < 2:
                    s2[i, j, s + 1] = total.astype(BF16)
                    p2_copy(i, j, s + 1).start()
                else:
                    gw_ref[
                        i * HALF_ROWS : (i + 1) * HALF_ROWS, j * HALF_COLS : (j + 1) * HALF_COLS
                    ] = total.astype(BF16)

    def output_part(image, j):
        rows = pl.ds(pl.multiple_of(image * PATCHES, PATCHES), PATCHES)
        total = None
        for o in range(NZ):
            panel = jnp.concatenate([aall[o * HEADS_HERE + h, rows] for h in range(HEADS_HERE)], axis=1)
            term = dot_nn(panel, weight_rows(j, o))
            total = term if total is None else total + term
        out_ref[rows, j * HALF_COLS : (j + 1) * HALF_COLS] = total.astype(BF16)

    for i, j in quarters:
        wall[j, y, x, core, i] = w_ref[
            i * HALF_ROWS : (i + 1) * HALF_ROWS, j * HALF_COLS : (j + 1) * HALF_COLS
        ]
    for i, j in quarters:
        w1_copy(i, j, 0).start()
    ws0_copy().start()

    def forward_loop(h, carry):
        for image in range(2):
            forward(image, h)
            a_copy(image, 0, h).start()
        for t in range(3):
            @pl.when(h == t)
            def _():
                weight_step(t)

        @pl.when(h >= 1)
        def _():
            a_pass(1, h - 1)

        return carry

    lax.fori_loop(0, HEADS_HERE, forward_loop, 0)
    a_pass(1, HEADS_HERE - 1)

    gw_block(0, gw_owner(0))

    def gather_loop(s, carry):
        for h in range(HEADS_HERE):
            a_pass(s, h)
        for t in range(3, 6):
            @pl.when(s == t - 1)
            def _():
                weight_step(t)

        @pl.when(s == 4)
        def _():
            gw_block(4, gw_owner(4))

        @pl.when(s >= 5)
        def _():
            def both(side, inner):
                index = jnp.where(side == 0, 8 - s, s)
                gw_block(index, gw_owner(index))
                return inner

            lax.fori_loop(0, 2, both, 0)

        return carry

    lax.fori_loop(2, 7, gather_loop, 0)
    weight_wait()
    g_first()
    for h in range(HEADS_HERE):
        for image in range(2):
            a_copy(image, 6, h).wait_recv()

    def last_two(side, carry):
        index = 1 + 6 * side
        gw_block(index, gw_owner(index))
        return carry

    lax.fori_loop(0, 2, last_two, 0)

    def reduce_loop(s, carry):
        g_step(s)

        @pl.when(s == 1)
        def _():
            for index in range(NZ):
                gw_copy(index, gw_owner(index)).wait_recv()

        for t in range(6):
            @pl.when(s == t + 1)
            def _():
                scatter_step(t)

        @pl.when(jnp.logical_and(s >= 2, s < 4))
        def _():
            for j in range(2):
                output_part(s - 2, j)

        return carry

    lax.fori_loop(1, 7, reduce_loop, 0)

    terms = [g_term(image, 7) for image in range(2)]
    for h in range(HEADS_HERE):
        for image in range(2):
            gsend[image, 7, h] = head_columns(terms[image], h).astype(BF16)

    def backward_loop(h, carry):
        for image in range(2):
            g_copy(image, 6, h).wait_recv()
            grad_attended = (gsend[image, 7, h].astype(F32) + grecv[image, 6, h].astype(F32)).astype(BF16)
            backward(image, h, grad_attended)

        @pl.when(h == 0)
        def _():
            scatter_step(6)

        return carry

    lax.fori_loop(0, HEADS_HERE, backward_loop, 0)

    weight_sent()
    for i, j in quarters:
        for s in range(3):
            p1_copy(i, j, s).wait_send()
            p2_copy(i, j, s).wait_send()
    for index in range(NZ):
        gw_copy(index, gw_owner(index)).wait_send()

    def sent_loop(s, carry):
        for h in range(HEADS_HERE):
            for image in range(2):
                a_copy(image, s, h).wait_send()
                g_copy(image, s, h).wait_send()
        return carry

    lax.fori_loop(0, 7, sent_loop, 0)


def per_device(queries, keys_in, values_in, query_gain, key_gain, out_weight, cotangent):
    dma = pltpu.SemaphoreType.DMA
    unit = (2, HEADS_HERE, PATCHES, HEAD_DIM)
    square = (2, HEADS_HERE, PATCHES, PATCHES)
    quarter = (HALF_ROWS, HALF_COLS)
    scratch = [
        pltpu.VMEM((2, NY, NX, 2, 2) + quarter, BF16),
        pltpu.VMEM((NZ * HEADS_HERE, 2 * PATCHES, HEAD_DIM), BF16),
        pltpu.VMEM(square, F32),
        pltpu.VMEM(square, BF16),
        pltpu.VMEM(unit, F32),
        pltpu.VMEM(unit, F32),
        pltpu.VMEM(unit, F32),
        pltpu.VMEM(unit, F32),
        pltpu.VMEM(unit, BF16),
        pltpu.VMEM(unit, BF16),
        pltpu.VMEM((2, 8, HEADS_HERE, PATCHES, HEAD_DIM), BF16),
        pltpu.VMEM((2, 7, HEADS_HERE, PATCHES, HEAD_DIM), BF16),
        pltpu.VMEM((2, NY, NX, 2, 2) + quarter, BF16),
        pltpu.VMEM((NY, NX, 2, 2) + quarter, BF16),
        pltpu.VMEM((2, 2, 3, 4) + quarter, BF16),
        pltpu.VMEM((2, 2, 3, 4) + quarter, BF16),
        pltpu.VMEM((2, 2, 3) + quarter, BF16),
        pltpu.VMEM((2, 2, 3) + quarter, BF16),
        pltpu.VMEM((2, 2, 4) + quarter, F32),
    ]
    ring4, ring8 = (2, 2, 3), (2, 7, HEADS_HERE)
    scratch += [dma(ring4), dma(ring4), dma(ring4), dma(ring4), dma, dma]
    scratch += [dma(ring4), dma(ring4), dma(ring4), dma(ring4)]
    scratch += [dma(ring8), dma(ring8), dma(ring8), dma(ring8), dma((NZ,)), dma((NZ,))]
    scratch += [dma(ring4), dma(ring4), dma(ring4), dma(ring4)]
    vmem = pl.BlockSpec(memory_space=pltpu.VMEM)
    gain_shape = (HEADS_HERE, 1, HEAD_DIM)
    tokens, features = queries.shape
    results = [
        jax.ShapeDtypeStruct(cotangent.shape, BF16),
        jax.ShapeDtypeStruct((tokens, features), BF16),
        jax.ShapeDtypeStruct((tokens, features), BF16),
        jax.ShapeDtypeStruct((tokens, features), BF16),
        jax.ShapeDtypeStruct(out_weight.shape, BF16),
    ]
    return pl.pallas_call(
        block_kernel,
        out_shape=results,
        in_specs=[vmem] * 7,
        out_specs=[vmem] * 5,
        scratch_shapes=scratch,
        compiler_params=pltpu.CompilerParams(
            collective_id=0, has_side_effects=True, vmem_limit_bytes=60 * 1024 * 1024
        ),
        cost_estimate=pl.CostEstimate(flops=8_000_000_000, bytes_accessed=4_200_000, transcendentals=400_000),
    )(
        queries,
        keys_in,
        values_in,
        query_gain.reshape(gain_shape),
        key_gain.reshape(gain_shape),
        out_weight,
        cotangent,
    )


def solution(mesh):
    placed = (
        P("row", "col"),
        P("row", "col"),
        P("row", "col"),
        P("col"),
        P("col"),
        P("row", "col"),
        P("row", "col"),
    )
    return jax.shard_map(
        per_device,
        mesh=mesh,
        in_specs=placed,
        out_specs=(P("row", "col"),) * 5,
        check_vma=False,
    )
```

```python
import jax
import jax.numpy as jnp
from jax import lax
from jax.experimental import pallas as pl
from jax.experimental.pallas import tpu as pltpu
from jax.sharding import PartitionSpec as P

HEAD_DIM = 128
PATCHES = 256
HEADS_HERE = 3
NX, NY, NZ = 4, 4, 8
SHARD_ROWS = 96
HALF_ROWS = 48
HALF_COLS = 384
TILE_ROWS = 128
PART_SLOTS = (((2, 5), (6, 7)), ((7, 8), (9, 12)))
PART_SHIFT = (3, 8)
STORE_PARTS = 2
EPSILON = 1e-06
MESH = pl.DeviceIdType.MESH
BF16 = jnp.bfloat16
F32 = jnp.float32


def dot_nn(a, b):
    return jnp.dot(a, b, preferred_element_type=F32)


def dot_nt(a, b):
    return lax.dot_general(a, b, (((1,), (1,)), ((), ())), preferred_element_type=F32)


def dot_tn(a, b):
    return lax.dot_general(a, b, (((0,), (0,)), ((), ())), preferred_element_type=F32)


def block_kernel(
    q_in, k_in, v_in, qg_in, kg_in, w_in, ct_in,
    out_hbm, gq_hbm, gk_hbm, gv_hbm, gw_hbm,
    q_ref, k_ref, v_ref, w_ref, ct_ref, qg_ref, kg_ref,
    out_ref, gq_ref, gk_ref, gv_ref, gw_ref,
    wall, aall, prob, plow, qhat, khat, qrs, krs, qn, kn,
    gsend, grecv, gterm, gwb, sib, s1, r1, s2, r2, c1,
    load_sem, out_sem, grad_sem, gw_sem,
    w1_send, w1_recv, w2_send, w2_recv, ws0_send, ws0_recv, ws1_send, ws1_recv, ws2_send, ws2_recv,
    a_send, a_recv, g_send, g_recv, sib_send, sib_recv, p1_send, p1_recv, p2_send, p2_recv,
):
    row = lax.axis_index("row")
    z = lax.axis_index("col")
    core = lax.rem(row, 2)
    x = lax.rem(lax.div(row, 2), NX)
    y = lax.div(row, 2 * NX)
    scale = HEAD_DIM ** (-0.5)

    def device(yy, xx, cc, zz):
        return ((yy * NX + xx) * 2 + cc, zz)

    def x_turn(j):
        return device(y, lax.rem(x + 1 + 2 * j, NX), core, z)

    def y_turn(j):
        return device(lax.rem(y + 1 + 2 * j, NY), x, core, z)

    def z_turn(image):
        return (row, lax.rem(z + 1 + 6 * image, NZ))

    sibling = device(y, x, 1 - core, z)

    barrier = pltpu.get_barrier_semaphore()
    for peer in (x_turn(0), x_turn(1), y_turn(0), y_turn(1), z_turn(0), z_turn(1), sibling):
        pl.semaphore_signal(barrier, inc=1, device_id=peer, device_id_type=MESH)

    loads = [
        pltpu.make_async_copy(source, target, load_sem.at[n])
        for n, (source, target) in enumerate(
            ((q_in, q_ref), (k_in, k_ref), (v_in, v_ref), (w_in, w_ref), (ct_in, ct_ref))
        )
    ]
    for load in loads:
        load.start()
    for h in range(HEADS_HERE):
        qg_ref[h, 0] = qg_in[h * HEAD_DIM : (h + 1) * HEAD_DIM]
        kg_ref[h, 0] = kg_in[h * HEAD_DIM : (h + 1) * HEAD_DIM]

    def remote(src, dst, send, recv, peer):
        return pltpu.make_async_remote_copy(
            src_ref=src, dst_ref=dst, send_sem=send, recv_sem=recv, device_id=peer, device_id_type=MESH
        )

    def behind(pos, steps, j):
        return lax.rem(pos + (4 - steps if j == 0 else steps), 4)

    def w1_ref(i, j, steps):
        if i == 0:
            return wall.at[j, y, behind(x, steps, j), core, i]
        return wall.at[j, behind(y, steps, j), x, core, i]

    def w2_ref(i, j, steps):
        if i == 0:
            return wall.at[j, behind(y, steps, j), :, core, i]
        return wall.at[j, :, behind(x, steps, j), core, i]

    def w1_copy(i, j, s):
        ref = w1_ref(i, j, s)
        return remote(ref, ref, w1_send.at[i, j, s], w1_recv.at[i, j, s], x_turn(j) if i == 0 else y_turn(j))

    def w2_copy(i, j, s):
        ref = w2_ref(i, j, s)
        return remote(ref, ref, w2_send.at[i, j, s], w2_recv.at[i, j, s], y_turn(j) if i == 0 else x_turn(j))

    def ws0_copy():
        ref = wall.at[:, y, x, core]
        return remote(ref, ref, ws0_send, ws0_recv, sibling)

    def ws1_copy(i, j, s):
        ref = w1_ref(i, j, s + 1)
        return remote(ref, ref, ws1_send.at[i, j, s], ws1_recv.at[i, j, s], sibling)

    def ws2_copy(i, j, s):
        ref = w2_ref(i, j, s + 1)
        return remote(ref, ref, ws2_send.at[i, j, s], ws2_recv.at[i, j, s], sibling)

    quarters = [(i, j) for i in range(2) for j in range(2)]

    def weight_step(t):
        for i, j in quarters:
            if t < 3:
                w1_copy(i, j, t).wait_recv()
                if t < 2:
                    w1_copy(i, j, t + 1).start()
                else:
                    w2_copy(i, j, 0).start()
                ws1_copy(i, j, t).start()
            else:
                w2_copy(i, j, t - 3).wait_recv()
                if t < 5:
                    w2_copy(i, j, t - 2).start()
                ws2_copy(i, j, t - 3).start()

    def weight_wait():
        ws0_copy().wait_recv()
        for i, j in quarters:
            for s in range(3):
                ws1_copy(i, j, s).wait_recv()
                ws2_copy(i, j, s).wait_recv()

    def weight_sent():
        ws0_copy().wait_send()
        for i, j in quarters:
            for s in range(3):
                w1_copy(i, j, s).wait_send()
                w2_copy(i, j, s).wait_send()
                ws1_copy(i, j, s).wait_send()
                ws2_copy(i, j, s).wait_send()

    def a_copy(image, s, h):
        origin = lax.rem(z + (NZ - s if image == 0 else s), NZ)
        ref = aall.at[origin * HEADS_HERE + h, pl.ds(image * PATCHES, PATCHES)]
        return remote(ref, ref, a_send.at[image, s, h], a_recv.at[image, s, h], z_turn(image))

    def a_pass(s, h):
        for image in range(2):
            a_copy(image, s - 1, h).wait_recv()
            a_copy(image, s, h).start()

    def head_slice(image, h):
        return (pl.ds(image * PATCHES, PATCHES), pl.ds(pl.multiple_of(h * HEAD_DIM, HEAD_DIM), HEAD_DIM))

    def norm_forward(image, h, source, gain, hat, spread_ref, normed):
        inside = source[head_slice(image, h)].astype(F32)
        centred = inside - jnp.mean(inside, axis=-1, keepdims=True)
        spread = jnp.mean(centred * centred, axis=-1, keepdims=True)
        factor = lax.rsqrt(spread + EPSILON)
        unit = centred * factor
        hat[image, h] = unit
        spread_ref[image, h] = jnp.broadcast_to(factor, unit.shape)
        value = (unit * gain[h]).astype(BF16)
        normed[image, h] = value
        return value

    def forward(image, h):
        q_norm = norm_forward(image, h, q_ref, qg_ref, qhat, qrs, qn)
        k_norm = norm_forward(image, h, k_ref, kg_ref, khat, krs, kn)
        weights = jnp.exp(dot_nt(q_norm, k_norm) * scale)
        probabilities = weights * (1.0 / jnp.sum(weights, axis=-1, keepdims=True))
        low = probabilities.astype(BF16)
        prob[image, h] = probabilities
        plow[image, h] = low
        attended = dot_nn(low, v_ref[head_slice(image, h)]).astype(BF16)
        aall[z * HEADS_HERE + h, pl.ds(image * PATCHES, PATCHES)] = attended

    def norm_backward(grad, image, h, gain, hat, spread_ref):
        scaled = grad * gain[h]
        unit = hat[image, h]
        first = jnp.mean(scaled, axis=-1, keepdims=True)
        second = jnp.mean(scaled * unit, axis=-1, keepdims=True)
        return (spread_ref[image, h] * (scaled - first - unit * second)).astype(BF16)

    def backward(image, h, grad_attended):
        place = head_slice(image, h)
        probabilities = prob[image, h]
        gv_ref[place] = dot_tn(plow[image, h], grad_attended).astype(BF16)
        grad_probs = dot_nt(grad_attended, v_ref[place])
        inner = jnp.sum(probabilities * grad_probs, axis=-1, keepdims=True)
        grad_scores = (probabilities * (grad_probs - inner) * scale).astype(BF16)
        grad_q = dot_nn(grad_scores, kn[image, h])
        grad_k = dot_tn(grad_scores, qn[image, h])
        gq_ref[place] = norm_backward(grad_q, image, h, qg_ref, qhat, qrs)
        gk_ref[place] = norm_backward(grad_k, image, h, kg_ref, khat, krs)

    def weight_rows(j, o):
        piece = wall[j, lax.div(o, 2), pl.ds(2 * lax.rem(o, 2), 2)]
        return piece.reshape(HEADS_HERE * HEAD_DIM, HALF_COLS)

    def g_copy(image, s, h):
        return remote(
            gsend.at[image, s, h], grecv.at[image, s, h], g_send.at[image, s, h], g_recv.at[image, s, h], z_turn(image)
        )

    def g_term(image, s):
        owner = lax.rem(z + (2 * NZ - 1 - s if image == 0 else 1 + s), NZ)
        rows = pl.ds(image * PATCHES, PATCHES)
        return dot_nt(ct_ref[rows, :HALF_COLS], weight_rows(0, owner)) + dot_nt(
            ct_ref[rows, HALF_COLS:], weight_rows(1, owner)
        )

    def head_columns(value, h):
        return value[:, h * HEAD_DIM : (h + 1) * HEAD_DIM]

    def g_first():
        for image in range(2):
            term = g_term(image, 0)
            for h in range(HEADS_HERE):
                gsend[image, 0, h] = head_columns(term, h).astype(BF16)
                g_copy(image, 0, h).start()

    def gw_copy(index, o):
        place = pl.ds(2 * lax.rem(o, 2), 2)
        return remote(
            gwb.at[1 - core, lax.div(o, 2), place],
            sib.at[lax.div(o, 2), place],
            sib_send.at[index],
            sib_recv.at[index],
            sibling,
        )

    def gw_block(index, o):
        panel = jnp.concatenate([aall[o * HEADS_HERE + h] for h in range(HEADS_HERE)], axis=1)
        for j in range(2):
            value = dot_tn(panel, ct_ref[:, j * HALF_COLS : (j + 1) * HALF_COLS]).astype(BF16)
            for xx in range(2):
                for cc in range(2):
                    for i in range(2):
                        at = (xx * 4 + cc * 2 + i) * HALF_ROWS
                        gwb[cc, lax.div(o, 2), 2 * lax.rem(o, 2) + xx, i, j] = value[at : at + HALF_ROWS]
        gw_copy(index, o).start()

    def gw_owner(index):
        return lax.rem(z + index, NZ)

    def chip_sum(i, j, d):
        if i == 0:
            return gwb[core, :, d, i, j].astype(F32) + sib[:, d, i, j].astype(F32)
        return gwb[core, d, :, i, j].astype(F32) + sib[d, :, i, j].astype(F32)

    def p1_copy(i, j, s):
        peer = x_turn(j) if i == 0 else y_turn(j)
        return remote(s1.at[i, j, s], r1.at[i, j, s], p1_send.at[i, j, s], p1_recv.at[i, j, s], peer)

    def p2_copy(i, j, s):
        peer = y_turn(j) if i == 0 else x_turn(j)
        return remote(s2.at[i, j, s], r2.at[i, j, s], p2_send.at[i, j, s], p2_recv.at[i, j, s], peer)

    def scatter_step(t):
        for i, j in quarters:
            first, second = (x, y) if i == 0 else (y, x)
            if t <= 3:
                total = chip_sum(i, j, behind(first, (1 + t) % 4, j))
                if t > 0:
                    p1_copy(i, j, t - 1).wait_recv()
                    total = total + r1[i, j, t - 1].astype(F32)
                if t < 3:
                    s1[i, j, t] = total.astype(BF16)
                    p1_copy(i, j, t).start()
                else:
                    c1[i, j] = total
                    s2[i, j, 0] = c1[i, j, behind(second, 1, j)].astype(BF16)
                    p2_copy(i, j, 0).start()
            else:
                s = t - 4
                p2_copy(i, j, s).wait_recv()
                total = c1[i, j, behind(second, (2 + s) % 4, j)] + r2[i, j, s].astype(F32)
                if s < 2:
                    s2[i, j, s + 1] = total.astype(BF16)
                    p2_copy(i, j, s + 1).start()
                else:
                    gw_ref[
                        i * HALF_ROWS : (i + 1) * HALF_ROWS, j * HALF_COLS : (j + 1) * HALF_COLS
                    ] = total.astype(BF16)

    def output_copy(tile):
        rows = pl.ds(pl.multiple_of(tile * TILE_ROWS, TILE_ROWS), TILE_ROWS)
        return pltpu.make_async_copy(out_ref.at[rows], out_hbm.at[rows], out_sem.at[tile])

    def output_part(tile, j):
        rows = pl.ds(pl.multiple_of(tile * TILE_ROWS, TILE_ROWS), TILE_ROWS)
        total = None
        for o in range(NZ):
            panel = jnp.concatenate([aall[o * HEADS_HERE + h, rows] for h in range(HEADS_HERE)], axis=1)
            term = dot_nn(panel, weight_rows(j, o))
            total = term if total is None else total + term
        out_ref[rows, j * HALF_COLS : (j + 1) * HALF_COLS] = total.astype(BF16)
        if j == 1:
            output_copy(tile).start()

    def grad_copies(h):
        columns = pl.ds(pl.multiple_of(h * HEAD_DIM, HEAD_DIM), HEAD_DIM)
        return [
            pltpu.make_async_copy(source.at[:, columns], target.at[:, columns], grad_sem.at[n, h])
            for n, (source, target) in enumerate(((gq_ref, gq_hbm), (gk_ref, gk_hbm), (gv_ref, gv_hbm)))
        ]

    loads[3].wait()
    for i, j in quarters:
        wall[j, y, x, core, i] = w_ref[
            i * HALF_ROWS : (i + 1) * HALF_ROWS, j * HALF_COLS : (j + 1) * HALF_COLS
        ]
    for load in loads[:3]:
        load.wait()
    pl.semaphore_wait(barrier, 7)
    for i, j in quarters:
        w1_copy(i, j, 0).start()
    ws0_copy().start()

    def at_slot(slot, moments, action):
        for t, moment in moments:
            @pl.when(slot == moment)
            def _():
                action(t)

    def forward_loop(h, carry):
        for image in range(2):
            forward(image, h)
            a_copy(image, 0, h).start()
        at_slot(h, ((0, 1), (1, 2)), weight_step)

        @pl.when(h >= 1)
        def _():
            a_pass(1, h - 1)

        return carry

    lax.fori_loop(0, HEADS_HERE, forward_loop, 0)
    loads[4].wait()
    a_pass(1, HEADS_HERE - 1)
    gw_block(0, gw_owner(0))

    def gather_loop(slot, carry):
        a_pass(2 + lax.div(slot, HEADS_HERE), lax.rem(slot, HEADS_HERE))
        at_slot(slot, ((2, 0), (3, 4), (4, 8), (5, 12)), weight_step)

        @pl.when(jnp.logical_or(slot == 9, jnp.logical_or(slot == 11, jnp.logical_or(slot == 13, slot == 14))))
        def _():
            index = jnp.where(slot == 9, 4, jnp.where(slot == 11, 3, jnp.where(slot == 13, 5, 2)))
            gw_block(index, gw_owner(index))

        return carry

    lax.fori_loop(0, 5 * HEADS_HERE, gather_loop, 0)
    weight_wait()
    g_first()
    for h in range(HEADS_HERE):
        for image in range(2):
            a_copy(image, 6, h).wait_recv()

    def last_three(n, carry):
        index = jnp.where(n == 0, 6, jnp.where(n == 1, 1, 7))
        gw_block(index, gw_owner(index))
        return carry

    lax.fori_loop(0, 3, last_three, 0)

    def reduce_loop(slot, carry):
        s, h = 1 + lax.div(slot, HEADS_HERE), lax.rem(slot, HEADS_HERE)

        @pl.when(h == 0)
        def _():
            for image in range(2):
                term = g_term(image, s)
                for head in range(HEADS_HERE):
                    gterm[image, head] = head_columns(term, head)

        for image in range(2):
            g_copy(image, s - 1, h).wait_recv()
            total = gterm[image, h] + grecv[image, s - 1, h].astype(F32)
            gsend[image, s, h] = total.astype(BF16)
            g_copy(image, s, h).start()

        @pl.when(slot == 1)
        def _():
            for index in range(NZ):
                gw_copy(index, gw_owner(index)).wait_recv()

        at_slot(slot, ((0, 1), (1, 5), (2, 8), (3, 12), (4, 14), (5, 16)), scatter_step)
        for j in range(2):

            @pl.when(jnp.logical_or(*[jnp.logical_and(slot >= a, slot < b) for a, b in PART_SLOTS[j]]))
            def _():
                output_part(slot - jnp.where(slot >= PART_SLOTS[j][1][0], PART_SHIFT[j], PART_SLOTS[j][0][0]), j)

        return carry

    lax.fori_loop(0, 6 * HEADS_HERE, reduce_loop, 0)

    for image in range(2):
        term = g_term(image, 7)
        for head in range(HEADS_HERE):
            gterm[image, head] = head_columns(term, head)

    def backward_loop(h, carry):
        for image in range(2):
            g_copy(image, 6, h).wait_recv()
            grad_attended = (gterm[image, h] + grecv[image, 6, h].astype(F32)).astype(BF16)
            backward(image, h, grad_attended)
        for copy in grad_copies(h):
            copy.start()

        @pl.when(h == 0)
        def _():
            scatter_step(6)
            gw_result = pltpu.make_async_copy(gw_ref, gw_hbm, gw_sem)
            gw_result.start()

        return carry

    lax.fori_loop(0, HEADS_HERE, backward_loop, 0)
    for h in range(HEADS_HERE):
        for copy in grad_copies(h):
            copy.wait()
    pltpu.make_async_copy(gw_ref, gw_hbm, gw_sem).wait()
    for tile in range(4):
        output_copy(tile).wait()

    weight_sent()
    for i, j in quarters:
        for s in range(3):
            p1_copy(i, j, s).wait_send()
            p2_copy(i, j, s).wait_send()
    for index in range(NZ):
        gw_copy(index, gw_owner(index)).wait_send()

    def sent_loop(s, carry):
        for h in range(HEADS_HERE):
            for image in range(2):
                a_copy(image, s, h).wait_send()
                g_copy(image, s, h).wait_send()
        return carry

    lax.fori_loop(0, 7, sent_loop, 0)


def store_kernel(*refs):
    made, results, held, load_sem, store_sem = refs[:5], refs[5:10], refs[10:15], refs[15], refs[16]
    parts = [(n, part) for n in range(5) for part in range(STORE_PARTS)]

    def piece(ref, part):
        rows = ref.shape[0] // STORE_PARTS
        return ref.at[pl.ds(part * rows, rows)]

    loads = [
        pltpu.make_async_copy(piece(made[n], part), piece(held[n], part), load_sem.at[n, part]) for n, part in parts
    ]
    stores = [
        pltpu.make_async_copy(piece(held[n], part), piece(results[n], part), store_sem.at[n, part])
        for n, part in parts
    ]
    for load in loads:
        load.start()
    for load, store in zip(loads, stores):
        load.wait()
        store.start()
    for store in stores:
        store.wait()


def per_device(queries, keys_in, values_in, query_gain, key_gain, out_weight, cotangent):
    dma = pltpu.SemaphoreType.DMA
    unit = (2, HEADS_HERE, PATCHES, HEAD_DIM)
    square = (2, HEADS_HERE, PATCHES, PATCHES)
    quarter = (HALF_ROWS, HALF_COLS)
    scratch = [pltpu.VMEM(a.shape, BF16) for a in (queries, keys_in, values_in, out_weight, cotangent)]
    scratch += [pltpu.VMEM((HEADS_HERE, 1, HEAD_DIM), F32)] * 2
    scratch += [pltpu.VMEM(a.shape, BF16) for a in (cotangent, queries, queries, queries, out_weight)]
    scratch += [
        pltpu.VMEM((2, NY, NX, 2, 2) + quarter, BF16),
        pltpu.VMEM((NZ * HEADS_HERE, 2 * PATCHES, HEAD_DIM), BF16),
        pltpu.VMEM(square, F32),
        pltpu.VMEM(square, BF16),
        pltpu.VMEM(unit, F32),
        pltpu.VMEM(unit, F32),
        pltpu.VMEM(unit, F32),
        pltpu.VMEM(unit, F32),
        pltpu.VMEM(unit, BF16),
        pltpu.VMEM(unit, BF16),
        pltpu.VMEM((2, 7, HEADS_HERE, PATCHES, HEAD_DIM), BF16),
        pltpu.VMEM((2, 7, HEADS_HERE, PATCHES, HEAD_DIM), BF16),
        pltpu.VMEM(unit, F32),
        pltpu.VMEM((2, NY, NX, 2, 2) + quarter, BF16),
        pltpu.VMEM((NY, NX, 2, 2) + quarter, BF16),
        pltpu.VMEM((2, 2, 3, 4) + quarter, BF16),
        pltpu.VMEM((2, 2, 3, 4) + quarter, BF16),
        pltpu.VMEM((2, 2, 3) + quarter, BF16),
        pltpu.VMEM((2, 2, 3) + quarter, BF16),
        pltpu.VMEM((2, 2, 4) + quarter, F32),
    ]
    ring4, ring8 = (2, 2, 3), (2, 7, HEADS_HERE)
    scratch += [dma((5,)), dma((4,)), dma((3, HEADS_HERE)), dma]
    scratch += [dma(ring4), dma(ring4), dma(ring4), dma(ring4), dma, dma]
    scratch += [dma(ring4), dma(ring4), dma(ring4), dma(ring4)]
    scratch += [dma(ring8), dma(ring8), dma(ring8), dma(ring8), dma((NZ,)), dma((NZ,))]
    scratch += [dma(ring4), dma(ring4), dma(ring4), dma(ring4)]
    vmem = pl.BlockSpec(memory_space=pltpu.VMEM)
    anywhere = pl.BlockSpec(memory_space=pl.ANY)
    tokens, features = queries.shape
    results = [
        jax.ShapeDtypeStruct(cotangent.shape, BF16),
        jax.ShapeDtypeStruct((tokens, features), BF16),
        jax.ShapeDtypeStruct((tokens, features), BF16),
        jax.ShapeDtypeStruct((tokens, features), BF16),
        jax.ShapeDtypeStruct(out_weight.shape, BF16),
    ]
    made = pl.pallas_call(
        block_kernel,
        out_shape=results,
        in_specs=[anywhere] * 3 + [vmem] * 2 + [anywhere] * 2,
        out_specs=[anywhere] * 5,
        scratch_shapes=scratch,
        compiler_params=pltpu.CompilerParams(
            collective_id=0, has_side_effects=True, vmem_limit_bytes=60 * 1024 * 1024
        ),
        cost_estimate=pl.CostEstimate(flops=8_000_000_000, bytes_accessed=4_200_000, transcendentals=400_000),
    )(
        queries, keys_in, values_in, query_gain, key_gain, out_weight, cotangent
    )
    return pl.pallas_call(
        store_kernel,
        out_shape=results,
        in_specs=[anywhere] * 5,
        out_specs=[anywhere] * 5,
        scratch_shapes=[pltpu.VMEM(a.shape, a.dtype) for a in results] + [dma((5, STORE_PARTS))] * 2,
        compiler_params=pltpu.CompilerParams(vmem_limit_bytes=60 * 1024 * 1024),
    )(*made)


def solution(mesh):
    placed = (
        P("row", "col"),
        P("row", "col"),
        P("row", "col"),
        P("col"),
        P("col"),
        P("row", "col"),
        P("row", "col"),
    )
    return jax.shard_map(
        per_device,
        mesh=mesh,
        in_specs=placed,
        out_specs=(P("row", "col"),) * 5,
        check_vma=False,
    )
```

```python
import jax
import jax.numpy as jnp
from jax import lax
from jax.experimental import pallas as pl
from jax.experimental.pallas import tpu as pltpu
from jax.sharding import PartitionSpec as P

HEAD_DIM = 128
PATCHES = 256
HEADS_HERE = 3
NX, NY, NZ = 4, 4, 8
SHARD_ROWS = 96
HALF_ROWS = 48
HALF_COLS = 384
TILE_ROWS = 128
PART_SLOTS = ((1, 2, 3, 5), (6, 7, 8, 10))
SCATTER_SLOTS = (0, 4, 9, 11, 13)
STORE_PARTS = 2
EPSILON = 1e-06
MESH = pl.DeviceIdType.MESH
BF16 = jnp.bfloat16
F32 = jnp.float32


def dot_nn(a, b):
    return jnp.dot(a, b, preferred_element_type=F32)


def dot_nt(a, b):
    return lax.dot_general(a, b, (((1,), (1,)), ((), ())), preferred_element_type=F32)


def dot_tn(a, b):
    return lax.dot_general(a, b, (((0,), (0,)), ((), ())), preferred_element_type=F32)


def block_kernel(
    q_in, k_in, v_in, qg_in, kg_in, w_in, ct_in,
    out_hbm, gq_hbm, gk_hbm, gv_hbm, gw_hbm,
    q_ref, k_ref, v_ref, w_ref, ct_ref, qg_ref, kg_ref,
    out_ref, gq_ref, gk_ref, gv_ref, gw_ref,
    wall, aall, prob, plow, qhat, khat, qrs, krs, qn, kn,
    gsend, grecv, gterm, gwb, sib, s1, r1, s2, r2, c1,
    load_sem, out_sem, grad_sem, gw_sem,
    w1_send, w1_recv, w2_send, w2_recv, ws0_send, ws0_recv, ws1_send, ws1_recv, ws2_send, ws2_recv,
    a_send, a_recv, g_send, g_recv, sib_send, sib_recv, p1_send, p1_recv, p2_send, p2_recv,
):
    row = lax.axis_index("row")
    z = lax.axis_index("col")
    core = lax.rem(row, 2)
    x = lax.rem(lax.div(row, 2), NX)
    y = lax.div(row, 2 * NX)
    scale = HEAD_DIM ** (-0.5)

    def device(yy, xx, cc, zz):
        return ((yy * NX + xx) * 2 + cc, zz)

    def x_turn(j):
        return device(y, lax.rem(x + 1 + 2 * j, NX), core, z)

    def y_turn(j):
        return device(lax.rem(y + 1 + 2 * j, NY), x, core, z)

    def z_turn(way):
        return (row, lax.rem(z + 1 + 6 * way, NZ))

    sibling = device(y, x, 1 - core, z)

    barrier = pltpu.get_barrier_semaphore()
    for peer in (x_turn(0), x_turn(1), y_turn(0), y_turn(1), z_turn(0), z_turn(1), sibling):
        pl.semaphore_signal(barrier, inc=1, device_id=peer, device_id_type=MESH)

    loads = [
        pltpu.make_async_copy(source, target, load_sem.at[n])
        for n, (source, target) in enumerate(
            ((q_in, q_ref), (k_in, k_ref), (v_in, v_ref), (w_in, w_ref), (ct_in, ct_ref))
        )
    ]
    for load in loads:
        load.start()
    for h in range(HEADS_HERE):
        qg_ref[h, 0] = qg_in[h * HEAD_DIM : (h + 1) * HEAD_DIM]
        kg_ref[h, 0] = kg_in[h * HEAD_DIM : (h + 1) * HEAD_DIM]

    def remote(src, dst, send, recv, peer):
        return pltpu.make_async_remote_copy(
            src_ref=src, dst_ref=dst, send_sem=send, recv_sem=recv, device_id=peer, device_id_type=MESH
        )

    def behind(pos, steps, j):
        return lax.rem(pos + (4 - steps if j == 0 else steps), 4)

    def w1_ref(i, j, steps):
        if i == 0:
            return wall.at[j, y, behind(x, steps, j), core, i]
        return wall.at[j, behind(y, steps, j), x, core, i]

    def w2_ref(i, j, steps):
        if i == 0:
            return wall.at[j, behind(y, steps, j), :, core, i]
        return wall.at[j, :, behind(x, steps, j), core, i]

    def w1_copy(i, j, s):
        ref = w1_ref(i, j, s)
        return remote(ref, ref, w1_send.at[i, j, s], w1_recv.at[i, j, s], x_turn(j) if i == 0 else y_turn(j))

    def w2_copy(i, j, s):
        ref = w2_ref(i, j, s)
        return remote(ref, ref, w2_send.at[i, j, s], w2_recv.at[i, j, s], y_turn(j) if i == 0 else x_turn(j))

    def ws0_copy():
        ref = wall.at[:, y, x, core]
        return remote(ref, ref, ws0_send, ws0_recv, sibling)

    def ws1_copy(i, j, s):
        ref = w1_ref(i, j, s + 1)
        return remote(ref, ref, ws1_send.at[i, j, s], ws1_recv.at[i, j, s], sibling)

    def ws2_copy(i, j, s):
        ref = w2_ref(i, j, s + 1)
        return remote(ref, ref, ws2_send.at[i, j, s], ws2_recv.at[i, j, s], sibling)

    quarters = [(i, j) for i in range(2) for j in range(2)]

    def weight_step(t):
        for i, j in quarters:
            if t < 3:
                w1_copy(i, j, t).wait_recv()
                if t < 2:
                    w1_copy(i, j, t + 1).start()
                else:
                    w2_copy(i, j, 0).start()
                ws1_copy(i, j, t).start()
            else:
                w2_copy(i, j, t - 3).wait_recv()
                if t < 5:
                    w2_copy(i, j, t - 2).start()
                ws2_copy(i, j, t - 3).start()

    def weight_wait():
        ws0_copy().wait_recv()
        for i, j in quarters:
            for s in range(3):
                ws1_copy(i, j, s).wait_recv()
                ws2_copy(i, j, s).wait_recv()

    def weight_sent():
        ws0_copy().wait_send()
        for i, j in quarters:
            for s in range(3):
                w1_copy(i, j, s).wait_send()
                w2_copy(i, j, s).wait_send()
                ws1_copy(i, j, s).wait_send()
                ws2_copy(i, j, s).wait_send()

    def image_rows(image):
        return pl.ds(pl.multiple_of(image * PATCHES, PATCHES), PATCHES)

    def a_copy(way, s, image, h):
        origin = lax.rem(z + (NZ - s if way == 0 else s), NZ)
        ref = aall.at[origin * HEADS_HERE + h, image_rows(image)]
        return remote(ref, ref, a_send.at[way, s, image, h], a_recv.at[way, s, image, h], z_turn(way))

    def a_own(image, h):
        for way in range(2):
            a_copy(way, 0, image, h).start()

    def a_pass(way, s, image, h):
        a_copy(way, s - 1, image, h).wait_recv()
        a_copy(way, s, image, h).start()

    def head_slice(image, h):
        return (pl.ds(image * PATCHES, PATCHES), pl.ds(pl.multiple_of(h * HEAD_DIM, HEAD_DIM), HEAD_DIM))

    def norm_forward(image, h, source, gain, hat, spread_ref, normed):
        inside = source[head_slice(image, h)].astype(F32)
        centred = inside - jnp.mean(inside, axis=-1, keepdims=True)
        spread = jnp.mean(centred * centred, axis=-1, keepdims=True)
        factor = lax.rsqrt(spread + EPSILON)
        unit = centred * factor
        hat[image, h] = unit
        spread_ref[image, h] = jnp.broadcast_to(factor, unit.shape)
        value = (unit * gain[h]).astype(BF16)
        normed[image, h] = value
        return value

    def forward(image, h):
        q_norm = norm_forward(image, h, q_ref, qg_ref, qhat, qrs, qn)
        k_norm = norm_forward(image, h, k_ref, kg_ref, khat, krs, kn)
        weights = jnp.exp(dot_nt(q_norm, k_norm) * scale)
        probabilities = weights * (1.0 / jnp.sum(weights, axis=-1, keepdims=True))
        low = probabilities.astype(BF16)
        prob[image, h] = probabilities
        plow[image, h] = low
        attended = dot_nn(low, v_ref[head_slice(image, h)]).astype(BF16)
        aall[z * HEADS_HERE + h, pl.ds(image * PATCHES, PATCHES)] = attended

    def norm_backward(grad, image, h, gain, hat, spread_ref):
        scaled = grad * gain[h]
        unit = hat[image, h]
        first = jnp.mean(scaled, axis=-1, keepdims=True)
        second = jnp.mean(scaled * unit, axis=-1, keepdims=True)
        return (spread_ref[image, h] * (scaled - first - unit * second)).astype(BF16)

    def backward(image, h, grad_attended):
        place = head_slice(image, h)
        probabilities = prob[image, h]
        gv_ref[place] = dot_tn(plow[image, h], grad_attended).astype(BF16)
        grad_probs = dot_nt(grad_attended, v_ref[place])
        inner = jnp.sum(probabilities * grad_probs, axis=-1, keepdims=True)
        grad_scores = (probabilities * (grad_probs - inner) * scale).astype(BF16)
        grad_q = dot_nn(grad_scores, kn[image, h])
        grad_k = dot_tn(grad_scores, qn[image, h])
        gq_ref[place] = norm_backward(grad_q, image, h, qg_ref, qhat, qrs)
        gk_ref[place] = norm_backward(grad_k, image, h, kg_ref, khat, krs)

    def weight_rows(j, o):
        piece = wall[j, lax.div(o, 2), pl.ds(2 * lax.rem(o, 2), 2)]
        return piece.reshape(HEADS_HERE * HEAD_DIM, HALF_COLS)

    def g_copy(way, s, image, h):
        at = (way, s, image, h)
        return remote(gsend.at[at], grecv.at[at], g_send.at[at], g_recv.at[at], z_turn(way))

    def g_term(owner):
        return dot_nt(ct_ref[:, :HALF_COLS], weight_rows(0, owner)) + dot_nt(
            ct_ref[:, HALF_COLS:], weight_rows(1, owner)
        )

    def g_part(term, image, h):
        return term[image * PATCHES : (image + 1) * PATCHES, h * HEAD_DIM : (h + 1) * HEAD_DIM]

    def g_owner(way, s):
        return lax.rem(z + (NZ + 4 - s if way == 0 else 4 + s), NZ)

    def g_make_term(way, s):
        term = g_term(g_owner(way, s))
        for image in range(2):
            for h in range(HEADS_HERE):
                gterm[s % 2, way, image, h] = g_part(term, image, h)

    def g_fresh(way, s, image, h, value):
        gsend[way, s, image, h] = value.astype(BF16)
        g_copy(way, s, image, h).start()

    def gw_copy(index, o):
        place = pl.ds(2 * lax.rem(o, 2), 2)
        return remote(
            gwb.at[1 - core, lax.div(o, 2), place],
            sib.at[lax.div(o, 2), place],
            sib_send.at[index],
            sib_recv.at[index],
            sibling,
        )

    def gw_block(index, o):
        panel = jnp.concatenate([aall[o * HEADS_HERE + h] for h in range(HEADS_HERE)], axis=1)
        product = dot_tn(panel, ct_ref[...]).astype(BF16)
        for j in range(2):
            value = product[:, j * HALF_COLS : (j + 1) * HALF_COLS]
            for xx in range(2):
                for cc in range(2):
                    for i in range(2):
                        at = (xx * 4 + cc * 2 + i) * HALF_ROWS
                        gwb[cc, lax.div(o, 2), 2 * lax.rem(o, 2) + xx, i, j] = value[at : at + HALF_ROWS]
        gw_copy(index, o).start()

    def gw_owner(index):
        return lax.rem(z + index, NZ)

    def chip_sum(i, j, d):
        if i == 0:
            return gwb[core, :, d, i, j].astype(F32) + sib[:, d, i, j].astype(F32)
        return gwb[core, d, :, i, j].astype(F32) + sib[d, :, i, j].astype(F32)

    def p1_copy(i, j, n):
        turn = 1 - j if n == 1 else j
        peer = x_turn(turn) if i == 0 else y_turn(turn)
        return remote(s1.at[i, j, n], r1.at[i, j, n], p1_send.at[i, j, n], p1_recv.at[i, j, n], peer)

    def p2_copy(i, j, n):
        turn = 1 - j if n == 1 else j
        peer = y_turn(turn) if i == 0 else x_turn(turn)
        return remote(s2.at[i, j, n], r2.at[i, j, n], p2_send.at[i, j, n], p2_recv.at[i, j, n], peer)

    def scatter_step(t):
        if t == 0:
            for n in range(2):
                for i, j in quarters:
                    s1[i, j, n] = chip_sum(i, j, behind(x if i == 0 else y, 2 - n, j)).astype(BF16)
                    p1_copy(i, j, n).start()
            return
        for i, j in quarters:
            first, second = (x, y) if i == 0 else (y, x)
            if t == 1:
                p1_copy(i, j, 0).wait_recv()
                total = chip_sum(i, j, behind(first, 3, j)) + r1[i, j, 0].astype(F32)
                s1[i, j, 2] = total.astype(BF16)
                p1_copy(i, j, 2).start()
            elif t == 2:
                total = chip_sum(i, j, first)
                for n in (1, 2):
                    p1_copy(i, j, n).wait_recv()
                    total = total + r1[i, j, n].astype(F32)
                c1[i, j] = total
                for n in range(2):
                    s2[i, j, n] = c1[i, j, behind(second, 2 - n, j)].astype(BF16)
                    p2_copy(i, j, n).start()
            elif t == 3:
                p2_copy(i, j, 0).wait_recv()
                total = c1[i, j, behind(second, 3, j)] + r2[i, j, 0].astype(F32)
                s2[i, j, 2] = total.astype(BF16)
                p2_copy(i, j, 2).start()
            else:
                total = c1[i, j, second]
                for n in (1, 2):
                    p2_copy(i, j, n).wait_recv()
                    total = total + r2[i, j, n].astype(F32)
                gw_ref[
                    i * HALF_ROWS : (i + 1) * HALF_ROWS, j * HALF_COLS : (j + 1) * HALF_COLS
                ] = total.astype(BF16)

    def output_copy(tile):
        rows = pl.ds(pl.multiple_of(tile * TILE_ROWS, TILE_ROWS), TILE_ROWS)
        return pltpu.make_async_copy(out_ref.at[rows], out_hbm.at[rows], out_sem.at[tile])

    def output_part(tile, j):
        rows = pl.ds(pl.multiple_of(tile * TILE_ROWS, TILE_ROWS), TILE_ROWS)
        total = None
        for o in range(NZ):
            panel = jnp.concatenate([aall[o * HEADS_HERE + h, rows] for h in range(HEADS_HERE)], axis=1)
            term = dot_nn(panel, weight_rows(j, o))
            total = term if total is None else total + term
        out_ref[rows, j * HALF_COLS : (j + 1) * HALF_COLS] = total.astype(BF16)
        if j == 1:
            output_copy(tile).start()

    def grad_copies(h):
        columns = pl.ds(pl.multiple_of(h * HEAD_DIM, HEAD_DIM), HEAD_DIM)
        return [
            pltpu.make_async_copy(source.at[:, columns], target.at[:, columns], grad_sem.at[n, h])
            for n, (source, target) in enumerate(((gq_ref, gq_hbm), (gk_ref, gk_hbm), (gv_ref, gv_hbm)))
        ]

    def gw_result():
        return pltpu.make_async_copy(gw_ref, gw_hbm, gw_sem)

    for load in loads[:3]:
        load.wait()
    forward(0, 0)
    pl.semaphore_wait(barrier, 7)
    a_own(0, 0)
    loads[3].wait()
    for i, j in quarters:
        wall[j, y, x, core, i] = w_ref[
            i * HALF_ROWS : (i + 1) * HALF_ROWS, j * HALF_COLS : (j + 1) * HALF_COLS
        ]
    for i, j in quarters:
        w1_copy(i, j, 0).start()
    ws0_copy().start()
    forward(1, 0)
    a_own(1, 0)

    def at_slot(slot, moments, action):
        for t, moment in moments:
            @pl.when(slot == moment)
            def _():
                action(t)

    def at_slot_of(slot, moments, action):
        hit, tile = slot == moments[0], jnp.where(slot == moments[0], 0, 0)
        for n, moment in enumerate(moments[1:]):
            hit, tile = jnp.logical_or(hit, slot == moment), jnp.where(slot == moment, n + 1, tile)

        @pl.when(hit)
        def _():
            action(tile)

    def forward_loop(h, carry):
        for image in range(2):
            forward(image, h)
            a_own(image, h)
        at_slot(h, ((0, 1), (1, 2)), weight_step)
        return carry

    lax.fori_loop(1, HEADS_HERE, forward_loop, 0)
    loads[4].wait()

    def block(index):
        gw_block(index, gw_owner(index))

    def gather_loop(slot, carry):
        k = lax.rem(slot, 6)
        for s in (1, 2):
            @pl.when(lax.div(slot, 6) == s - 1)
            def _():
                for way in range(2):
                    a_pass(way, s, lax.rem(k, 2), lax.div(k, 2))

        at_slot(slot, ((2, 1), (3, 4), (4, 7), (5, 10)), weight_step)

        @pl.when(jnp.logical_or(slot == 2, jnp.logical_or(slot == 6, slot == 8)))
        def _():
            block(jnp.where(slot == 2, 0, jnp.where(slot == 6, 1, 7)))

        return carry

    lax.fori_loop(0, 12, gather_loop, 0)

    def last_hop_loop(h, carry):
        for way in range(2):
            a_pass(way, 3, way, h)

        @pl.when(h < 2)
        def _():
            block(2 + 4 * h)

        return carry

    lax.fori_loop(0, HEADS_HERE, last_hop_loop, 0)
    weight_wait()
    term = g_term(g_owner(0, 0))
    for h in range(HEADS_HERE):
        for way in range(2):
            g_fresh(way, 0, way, h, g_part(term, way, h))
    for h in range(HEADS_HERE):
        for way in range(2):
            a_copy(way, 2, 1 - way, h).wait_recv()

    def third_hop_loop(n, carry):
        block(3 + 2 * n)
        return carry

    lax.fori_loop(0, 2, third_hop_loop, 0)
    for way in range(2):
        g_make_term(way, 1)
    for h in range(HEADS_HERE):
        for way in range(2):
            g_fresh(way, 1, 1 - way, h, gterm[1, way, 1 - way, h])
    for h in range(HEADS_HERE):
        for way in range(2):
            a_copy(way, 3, way, h).wait_recv()
    block(4)

    def reduce_loop(slot, carry):
        s, k = 1 + lax.div(slot + 3, 6), lax.rem(slot + 3, 6)
        h = jnp.where(slot < 3, slot, lax.div(k, 2))
        for way in range(2):
            image = jnp.where(slot < 3, way, lax.rem(k, 2))
            g_copy(way, s - 1, image, h).wait_recv()
            total = gterm[lax.rem(s, 2), way, image, h] + grecv[way, s - 1, image, h].astype(F32)
            g_fresh(way, s, image, h, total)

        @pl.when(slot == SCATTER_SLOTS[0])
        def _():
            for index in range(NZ):
                gw_copy(index, gw_owner(index)).wait_recv()

        at_slot(slot, tuple(enumerate(SCATTER_SLOTS)), scatter_step)
        for moment, way, step in ((1, 0, 2), (2, 1, 2), (5, 0, 3), (7, 1, 3), (11, 0, 4)):
            @pl.when(slot == moment)
            def _():
                g_make_term(way, step)

        for j in range(2):
            at_slot_of(slot, PART_SLOTS[j], lambda tile: output_part(tile, j))

        @pl.when(slot == SCATTER_SLOTS[4])
        def _():
            gw_result().start()
            for i, j in quarters:
                for n in range(3):
                    p1_copy(i, j, n).wait_send()
            for index in range(NZ):
                gw_copy(index, gw_owner(index)).wait_send()

        @pl.when(slot == 10)
        def _():
            weight_sent()

        @pl.when(slot == 12)
        def _():
            for way, s, image, h in gather_chunks:
                a_copy(way, s, image, h).wait_send()

        @pl.when(slot == 14)
        def _():
            for way, s, image, h in reduce_chunks:
                if s < 2:
                    g_copy(way, s, image, h).wait_send()

        return carry

    chunks = [(way, image, h) for way in range(2) for image in range(2) for h in range(HEADS_HERE)]
    gather_chunks = [(way, s, image, h) for s in range(4) for way, image, h in chunks if s < 3 or way == image]
    reduce_chunks = [(way, s, image, h) for s in range(4) for way, image, h in chunks if s > 0 or way == image]
    lax.fori_loop(0, 15, reduce_loop, 0)

    def backward_loop(h, carry):
        for image in range(2):
            total = gterm[0, 0, image, h]
            for way in range(2):
                g_copy(way, 3, image, h).wait_recv()
                total = total + grecv[way, 3, image, h].astype(F32)
            backward(image, h, total.astype(BF16))
        for copy in grad_copies(h):
            copy.start()

        return carry

    lax.fori_loop(0, HEADS_HERE, backward_loop, 0)

    for way, s, image, h in reduce_chunks:
        if s >= 2:
            g_copy(way, s, image, h).wait_send()
    for i, j in quarters:
        for s in range(3):
            p2_copy(i, j, s).wait_send()
    for tile in range(4):
        output_copy(tile).wait()
    gw_result().wait()
    for h in range(HEADS_HERE):
        for copy in grad_copies(h):
            copy.wait()


def store_kernel(*refs):
    made, results, held, load_sem, store_sem = refs[:5], refs[5:10], refs[10:15], refs[15], refs[16]
    parts = [(n, part) for n in range(5) for part in range(STORE_PARTS)]

    def piece(ref, part):
        rows = ref.shape[0] // STORE_PARTS
        return ref.at[pl.ds(part * rows, rows)]

    loads = [
        pltpu.make_async_copy(piece(made[n], part), piece(held[n], part), load_sem.at[n, part]) for n, part in parts
    ]
    stores = [
        pltpu.make_async_copy(piece(held[n], part), piece(results[n], part), store_sem.at[n, part])
        for n, part in parts
    ]
    for load in loads:
        load.start()
    for load, store in zip(loads, stores):
        load.wait()
        store.start()
    for store in stores:
        store.wait()


def per_device(queries, keys_in, values_in, query_gain, key_gain, out_weight, cotangent):
    dma = pltpu.SemaphoreType.DMA
    unit = (2, HEADS_HERE, PATCHES, HEAD_DIM)
    square = (2, HEADS_HERE, PATCHES, PATCHES)
    quarter = (HALF_ROWS, HALF_COLS)
    scratch = [pltpu.VMEM(a.shape, BF16) for a in (queries, keys_in, values_in, out_weight, cotangent)]
    scratch += [pltpu.VMEM((HEADS_HERE, 1, HEAD_DIM), F32)] * 2
    scratch += [pltpu.VMEM(a.shape, BF16) for a in (cotangent, queries, queries, queries, out_weight)]
    scratch += [
        pltpu.VMEM((2, NY, NX, 2, 2) + quarter, BF16),
        pltpu.VMEM((NZ * HEADS_HERE, 2 * PATCHES, HEAD_DIM), BF16),
        pltpu.VMEM(square, F32),
        pltpu.VMEM(square, BF16),
        pltpu.VMEM(unit, F32),
        pltpu.VMEM(unit, F32),
        pltpu.VMEM(unit, F32),
        pltpu.VMEM(unit, F32),
        pltpu.VMEM(unit, BF16),
        pltpu.VMEM(unit, BF16),
        pltpu.VMEM((2, 4) + unit, BF16),
        pltpu.VMEM((2, 4) + unit, BF16),
        pltpu.VMEM((2, 2) + unit, F32),
        pltpu.VMEM((2, NY, NX, 2, 2) + quarter, BF16),
        pltpu.VMEM((NY, NX, 2, 2) + quarter, BF16),
        pltpu.VMEM((2, 2, 3, 4) + quarter, BF16),
        pltpu.VMEM((2, 2, 3, 4) + quarter, BF16),
        pltpu.VMEM((2, 2, 3) + quarter, BF16),
        pltpu.VMEM((2, 2, 3) + quarter, BF16),
        pltpu.VMEM((2, 2, 4) + quarter, F32),
    ]
    ring4, ring8 = (2, 2, 3), (2, 4, 2, HEADS_HERE)
    scratch += [dma((5,)), dma((4,)), dma((3, HEADS_HERE)), dma]
    scratch += [dma(ring4), dma(ring4), dma(ring4), dma(ring4), dma, dma]
    scratch += [dma(ring4), dma(ring4), dma(ring4), dma(ring4)]
    scratch += [dma(ring8), dma(ring8), dma(ring8), dma(ring8), dma((NZ,)), dma((NZ,))]
    scratch += [dma(ring4), dma(ring4), dma(ring4), dma(ring4)]
    vmem = pl.BlockSpec(memory_space=pltpu.VMEM)
    anywhere = pl.BlockSpec(memory_space=pl.ANY)
    tokens, features = queries.shape
    results = [
        jax.ShapeDtypeStruct(cotangent.shape, BF16),
        jax.ShapeDtypeStruct((tokens, features), BF16),
        jax.ShapeDtypeStruct((tokens, features), BF16),
        jax.ShapeDtypeStruct((tokens, features), BF16),
        jax.ShapeDtypeStruct(out_weight.shape, BF16),
    ]
    made = pl.pallas_call(
        block_kernel,
        out_shape=results,
        in_specs=[anywhere] * 3 + [vmem] * 2 + [anywhere] * 2,
        out_specs=[anywhere] * 5,
        scratch_shapes=scratch,
        compiler_params=pltpu.CompilerParams(
            collective_id=0, has_side_effects=True, vmem_limit_bytes=60 * 1024 * 1024
        ),
        cost_estimate=pl.CostEstimate(flops=8_000_000_000, bytes_accessed=4_200_000, transcendentals=400_000),
    )(
        queries, keys_in, values_in, query_gain, key_gain, out_weight, cotangent
    )
    return pl.pallas_call(
        store_kernel,
        out_shape=results,
        in_specs=[anywhere] * 5,
        out_specs=[anywhere] * 5,
        scratch_shapes=[pltpu.VMEM(a.shape, a.dtype) for a in results] + [dma((5, STORE_PARTS))] * 2,
        compiler_params=pltpu.CompilerParams(vmem_limit_bytes=60 * 1024 * 1024),
    )(*made)


def solution(mesh):
    placed = (
        P("row", "col"),
        P("row", "col"),
        P("row", "col"),
        P("col"),
        P("col"),
        P("row", "col"),
        P("row", "col"),
    )
    return jax.shard_map(
        per_device,
        mesh=mesh,
        in_specs=placed,
        out_specs=(P("row", "col"),) * 5,
        check_vma=False,
    )
```

```python
import jax
import jax.numpy as jnp
from jax import lax
from jax.experimental import pallas as pl
from jax.experimental.pallas import tpu as pltpu
from jax.sharding import PartitionSpec as P

HEAD_DIM = 128
PATCHES = 256
HEADS_HERE = 3
NX, NY, NZ = 4, 4, 8
SHARD_ROWS = 96
HALF_ROWS = 48
HALF_COLS = 384
TILE_ROWS = 128
PART_SLOTS = ((1, 2, 3, 5), (6, 7, 8, 10))
SCATTER_SLOTS = (0, 4, 9, 11, 13)
STORE_PARTS = 2
EPSILON = 1e-06
MESH = pl.DeviceIdType.MESH
BF16 = jnp.bfloat16
F32 = jnp.float32


def dot_nn(a, b):
    return jnp.dot(a, b, preferred_element_type=F32)


def dot_nt(a, b):
    return lax.dot_general(a, b, (((1,), (1,)), ((), ())), preferred_element_type=F32)


def dot_tn(a, b):
    return lax.dot_general(a, b, (((0,), (0,)), ((), ())), preferred_element_type=F32)


def block_kernel(
    q_in, k_in, v_in, qg_in, kg_in, w_in, ct_in,
    out_hbm, gq_hbm, gk_hbm, gv_hbm, gw_hbm,
    q_ref, k_ref, v_ref, w_ref, ct_ref, qg_ref, kg_ref,
    out_ref, gq_ref, gk_ref, gv_ref, gw_ref,
    wall, aall, prob, plow, qhat, khat, qrs, krs, qn, kn,
    gsend, grecv, gterm, gwb, sib, s1, r1, s2, r2, c1,
    load_sem, out_sem, grad_sem, gw_sem,
    w1_send, w1_recv, w2_send, w2_recv, ws0_send, ws0_recv, ws1_send, ws1_recv, ws2_send, ws2_recv,
    a_send, a_recv, g_send, g_recv, sib_send, sib_recv, p1_send, p1_recv, p2_send, p2_recv,
):
    row = lax.axis_index("row")
    z = lax.axis_index("col")
    core = lax.rem(row, 2)
    x = lax.rem(lax.div(row, 2), NX)
    y = lax.div(row, 2 * NX)
    scale = HEAD_DIM ** (-0.5)

    def device(yy, xx, cc, zz):
        return ((yy * NX + xx) * 2 + cc, zz)

    def x_turn(j):
        return device(y, lax.rem(x + 1 + 2 * j, NX), core, z)

    def y_turn(j):
        return device(lax.rem(y + 1 + 2 * j, NY), x, core, z)

    def z_turn(way):
        return (row, lax.rem(z + 1 + 6 * way, NZ))

    sibling = device(y, x, 1 - core, z)

    barrier = pltpu.get_barrier_semaphore()
    for peer in (x_turn(0), x_turn(1), y_turn(0), y_turn(1), z_turn(0), z_turn(1), sibling):
        pl.semaphore_signal(barrier, inc=1, device_id=peer, device_id_type=MESH)

    loads = [
        pltpu.make_async_copy(source, target, load_sem.at[n])
        for n, (source, target) in enumerate(
            ((q_in, q_ref), (k_in, k_ref), (v_in, v_ref), (w_in, w_ref), (ct_in, ct_ref))
        )
    ]
    for load in loads:
        load.start()
    for h in range(HEADS_HERE):
        qg_ref[h, 0] = qg_in[h * HEAD_DIM : (h + 1) * HEAD_DIM]
        kg_ref[h, 0] = kg_in[h * HEAD_DIM : (h + 1) * HEAD_DIM]

    def remote(src, dst, send, recv, peer):
        return pltpu.make_async_remote_copy(
            src_ref=src, dst_ref=dst, send_sem=send, recv_sem=recv, device_id=peer, device_id_type=MESH
        )

    def behind(pos, steps, j):
        return lax.rem(pos + (4 - steps if j == 0 else steps), 4)

    def w1_ref(i, j, steps):
        if i == 0:
            return wall.at[j, y, behind(x, steps, j), core, i]
        return wall.at[j, behind(y, steps, j), x, core, i]

    def w2_ref(i, j, steps):
        if i == 0:
            return wall.at[j, behind(y, steps, j), :, core, i]
        return wall.at[j, :, behind(x, steps, j), core, i]

    def w1_copy(i, j, s):
        ref = w1_ref(i, j, s)
        return remote(ref, ref, w1_send.at[i, j, s], w1_recv.at[i, j, s], x_turn(j) if i == 0 else y_turn(j))

    def w2_copy(i, j, s):
        ref = w2_ref(i, j, s)
        return remote(ref, ref, w2_send.at[i, j, s], w2_recv.at[i, j, s], y_turn(j) if i == 0 else x_turn(j))

    def ws0_copy():
        ref = wall.at[:, y, x, core]
        return remote(ref, ref, ws0_send, ws0_recv, sibling)

    def ws1_copy(i, j, s):
        ref = w1_ref(i, j, s + 1)
        return remote(ref, ref, ws1_send.at[i, j, s], ws1_recv.at[i, j, s], sibling)

    def ws2_copy(i, j, s):
        ref = w2_ref(i, j, s + 1)
        return remote(ref, ref, ws2_send.at[i, j, s], ws2_recv.at[i, j, s], sibling)

    quarters = [(i, j) for i in range(2) for j in range(2)]

    def weight_step(t):
        for i, j in quarters:
            if t < 3:
                w1_copy(i, j, t).wait_recv()
                if t < 2:
                    w1_copy(i, j, t + 1).start()
                else:
                    w2_copy(i, j, 0).start()
                ws1_copy(i, j, t).start()
            else:
                w2_copy(i, j, t - 3).wait_recv()
                if t < 5:
                    w2_copy(i, j, t - 2).start()
                ws2_copy(i, j, t - 3).start()

    def weight_wait():
        ws0_copy().wait_recv()
        for i, j in quarters:
            for s in range(3):
                ws1_copy(i, j, s).wait_recv()
                ws2_copy(i, j, s).wait_recv()

    def weight_sent():
        ws0_copy().wait_send()
        for i, j in quarters:
            for s in range(3):
                w1_copy(i, j, s).wait_send()
                w2_copy(i, j, s).wait_send()
                ws1_copy(i, j, s).wait_send()
                ws2_copy(i, j, s).wait_send()

    def image_rows(image):
        return pl.ds(pl.multiple_of(image * PATCHES, PATCHES), PATCHES)

    def a_copy(way, s, image, h):
        origin = lax.rem(z + (NZ - s if way == 0 else s), NZ)
        ref = aall.at[origin * HEADS_HERE + h, image_rows(image)]
        return remote(ref, ref, a_send.at[way, s, image, h], a_recv.at[way, s, image, h], z_turn(way))

    def a_own(image, h):
        for way in range(2):
            a_copy(way, 0, image, h).start()

    def a_pair(way, s, h):
        origin = lax.rem(z + (NZ - s if way == 0 else s), NZ)
        ref = aall.at[origin * HEADS_HERE + h]
        return remote(ref, ref, a_send.at[way, s, 0, h], a_recv.at[way, s, 0, h], z_turn(way))

    def head_slice(image, h):
        return (pl.ds(image * PATCHES, PATCHES), pl.ds(pl.multiple_of(h * HEAD_DIM, HEAD_DIM), HEAD_DIM))

    def norm_forward(image, h, source, gain, hat, spread_ref, normed):
        inside = source[head_slice(image, h)].astype(F32)
        centred = inside - jnp.mean(inside, axis=-1, keepdims=True)
        spread = jnp.mean(centred * centred, axis=-1, keepdims=True)
        factor = lax.rsqrt(spread + EPSILON)
        unit = centred * factor
        hat[image, h] = unit
        spread_ref[image, h] = jnp.broadcast_to(factor, unit.shape)
        value = (unit * gain[h]).astype(BF16)
        normed[image, h] = value
        return value

    def forward(image, h):
        q_norm = norm_forward(image, h, q_ref, qg_ref, qhat, qrs, qn)
        k_norm = norm_forward(image, h, k_ref, kg_ref, khat, krs, kn)
        weights = jnp.exp(dot_nt(q_norm, k_norm) * scale)
        probabilities = weights * (1.0 / jnp.sum(weights, axis=-1, keepdims=True))
        low = probabilities.astype(BF16)
        prob[image, h] = probabilities
        plow[image, h] = low
        attended = dot_nn(low, v_ref[head_slice(image, h)]).astype(BF16)
        aall[z * HEADS_HERE + h, pl.ds(image * PATCHES, PATCHES)] = attended

    def norm_backward(grad, image, h, gain, hat, spread_ref):
        scaled = grad * gain[h]
        unit = hat[image, h]
        first = jnp.mean(scaled, axis=-1, keepdims=True)
        second = jnp.mean(scaled * unit, axis=-1, keepdims=True)
        return (spread_ref[image, h] * (scaled - first - unit * second)).astype(BF16)

    def backward(image, h, grad_attended):
        place = head_slice(image, h)
        probabilities = prob[image, h]
        gv_ref[place] = dot_tn(plow[image, h], grad_attended).astype(BF16)
        grad_probs = dot_nt(grad_attended, v_ref[place])
        inner = jnp.sum(probabilities * grad_probs, axis=-1, keepdims=True)
        grad_scores = (probabilities * (grad_probs - inner) * scale).astype(BF16)
        grad_q = dot_nn(grad_scores, kn[image, h])
        grad_k = dot_tn(grad_scores, qn[image, h])
        gq_ref[place] = norm_backward(grad_q, image, h, qg_ref, qhat, qrs)
        gk_ref[place] = norm_backward(grad_k, image, h, kg_ref, khat, krs)

    def weight_rows(j, o):
        piece = wall[j, lax.div(o, 2), pl.ds(2 * lax.rem(o, 2), 2)]
        return piece.reshape(HEADS_HERE * HEAD_DIM, HALF_COLS)

    def g_copy(way, s, image, h):
        at = (way, s, image, h)
        return remote(gsend.at[at], grecv.at[at], g_send.at[at], g_recv.at[at], z_turn(way))

    def g_term(owner):
        return dot_nt(ct_ref[:, :HALF_COLS], weight_rows(0, owner)) + dot_nt(
            ct_ref[:, HALF_COLS:], weight_rows(1, owner)
        )

    def g_part(term, image, h):
        return term[image * PATCHES : (image + 1) * PATCHES, h * HEAD_DIM : (h + 1) * HEAD_DIM]

    def g_owner(way, s):
        return lax.rem(z + (NZ + 4 - s if way == 0 else 4 + s), NZ)

    def g_make_term(way, s):
        term = g_term(g_owner(way, s))
        for image in range(2):
            for h in range(HEADS_HERE):
                gterm[s % 2, way, image, h] = g_part(term, image, h)

    def g_fresh(way, s, image, h, value):
        gsend[way, s, image, h] = value.astype(BF16)
        g_copy(way, s, image, h).start()

    def gw_copy(index, o):
        place = pl.ds(2 * lax.rem(o, 2), 2)
        return remote(
            gwb.at[1 - core, lax.div(o, 2), place],
            sib.at[lax.div(o, 2), place],
            sib_send.at[index],
            sib_recv.at[index],
            sibling,
        )

    def gw_block(index, o):
        panel = jnp.concatenate([aall[o * HEADS_HERE + h] for h in range(HEADS_HERE)], axis=1)
        product = dot_tn(panel, ct_ref[...]).astype(BF16)
        for j in range(2):
            value = product[:, j * HALF_COLS : (j + 1) * HALF_COLS]
            for xx in range(2):
                for cc in range(2):
                    for i in range(2):
                        at = (xx * 4 + cc * 2 + i) * HALF_ROWS
                        gwb[cc, lax.div(o, 2), 2 * lax.rem(o, 2) + xx, i, j] = value[at : at + HALF_ROWS]
        gw_copy(index, o).start()

    def gw_owner(index):
        return lax.rem(z + index, NZ)

    def chip_sum(i, j, d):
        if i == 0:
            return gwb[core, :, d, i, j].astype(F32) + sib[:, d, i, j].astype(F32)
        return gwb[core, d, :, i, j].astype(F32) + sib[d, :, i, j].astype(F32)

    def p1_copy(i, j, n):
        turn = 1 - j if n == 1 else j
        peer = x_turn(turn) if i == 0 else y_turn(turn)
        return remote(s1.at[i, j, n], r1.at[i, j, n], p1_send.at[i, j, n], p1_recv.at[i, j, n], peer)

    def p2_copy(i, j, n):
        turn = 1 - j if n == 1 else j
        peer = y_turn(turn) if i == 0 else x_turn(turn)
        return remote(s2.at[i, j, n], r2.at[i, j, n], p2_send.at[i, j, n], p2_recv.at[i, j, n], peer)

    def scatter_step(t):
        if t == 0:
            for n in range(2):
                for i, j in quarters:
                    s1[i, j, n] = chip_sum(i, j, behind(x if i == 0 else y, 2 - n, j)).astype(BF16)
                    p1_copy(i, j, n).start()
            return
        for i, j in quarters:
            first, second = (x, y) if i == 0 else (y, x)
            if t == 1:
                p1_copy(i, j, 0).wait_recv()
                total = chip_sum(i, j, behind(first, 3, j)) + r1[i, j, 0].astype(F32)
                s1[i, j, 2] = total.astype(BF16)
                p1_copy(i, j, 2).start()
            elif t == 2:
                total = chip_sum(i, j, first)
                for n in (1, 2):
                    p1_copy(i, j, n).wait_recv()
                    total = total + r1[i, j, n].astype(F32)
                c1[i, j] = total
                for n in range(2):
                    s2[i, j, n] = c1[i, j, behind(second, 2 - n, j)].astype(BF16)
                    p2_copy(i, j, n).start()
            elif t == 3:
                p2_copy(i, j, 0).wait_recv()
                total = c1[i, j, behind(second, 3, j)] + r2[i, j, 0].astype(F32)
                s2[i, j, 2] = total.astype(BF16)
                p2_copy(i, j, 2).start()
            else:
                total = c1[i, j, second]
                for n in (1, 2):
                    p2_copy(i, j, n).wait_recv()
                    total = total + r2[i, j, n].astype(F32)
                gw_ref[
                    i * HALF_ROWS : (i + 1) * HALF_ROWS, j * HALF_COLS : (j + 1) * HALF_COLS
                ] = total.astype(BF16)

    def output_copy(tile):
        rows = pl.ds(pl.multiple_of(tile * TILE_ROWS, TILE_ROWS), TILE_ROWS)
        return pltpu.make_async_copy(out_ref.at[rows], out_hbm.at[rows], out_sem.at[tile])

    def output_part(tile, j):
        rows = pl.ds(pl.multiple_of(tile * TILE_ROWS, TILE_ROWS), TILE_ROWS)
        total = None
        for o in range(NZ):
            panel = jnp.concatenate([aall[o * HEADS_HERE + h, rows] for h in range(HEADS_HERE)], axis=1)
            term = dot_nn(panel, weight_rows(j, o))
            total = term if total is None else total + term
        out_ref[rows, j * HALF_COLS : (j + 1) * HALF_COLS] = total.astype(BF16)
        if j == 1:
            output_copy(tile).start()

    def grad_copies(h):
        columns = pl.ds(pl.multiple_of(h * HEAD_DIM, HEAD_DIM), HEAD_DIM)
        return [
            pltpu.make_async_copy(source.at[:, columns], target.at[:, columns], grad_sem.at[n, h])
            for n, (source, target) in enumerate(((gq_ref, gq_hbm), (gk_ref, gk_hbm), (gv_ref, gv_hbm)))
        ]

    def gw_result():
        return pltpu.make_async_copy(gw_ref, gw_hbm, gw_sem)

    for load in loads[:3]:
        load.wait()
    forward(0, 0)
    pl.semaphore_wait(barrier, 7)
    a_own(0, 0)
    loads[3].wait()
    for i, j in quarters:
        wall[j, y, x, core, i] = w_ref[
            i * HALF_ROWS : (i + 1) * HALF_ROWS, j * HALF_COLS : (j + 1) * HALF_COLS
        ]
    for i, j in quarters:
        w1_copy(i, j, 0).start()
    ws0_copy().start()
    forward(1, 0)
    a_own(1, 0)

    def at_slot(slot, moments, action):
        for t, moment in moments:
            @pl.when(slot == moment)
            def _():
                action(t)

    def at_slot_of(slot, moments, action):
        hit, tile = slot == moments[0], jnp.where(slot == moments[0], 0, 0)
        for n, moment in enumerate(moments[1:]):
            hit, tile = jnp.logical_or(hit, slot == moment), jnp.where(slot == moment, n + 1, tile)

        @pl.when(hit)
        def _():
            action(tile)

    def forward_loop(h, carry):
        for image in range(2):
            forward(image, h)
            a_own(image, h)
        at_slot(h, ((0, 1), (1, 2)), weight_step)
        return carry

    lax.fori_loop(1, HEADS_HERE, forward_loop, 0)
    loads[4].wait()

    def block(index):
        gw_block(index, gw_owner(index))

    def gather_loop(slot, carry):
        k = lax.rem(slot, 6)
        for s in (1, 2):
            @pl.when(lax.div(slot, 6) == s - 1)
            def _():
                @pl.when(lax.rem(k, 2) == 0)
                def _():
                    h = lax.div(k, 2)
                    for way in range(2):
                        if s == 1:
                            for image in range(2):
                                a_copy(way, 0, image, h).wait_recv()
                        else:
                            a_pair(way, 1, h).wait_recv()
                        a_pair(way, s, h).start()

        at_slot(slot, ((2, 1), (3, 4), (4, 7), (5, 10)), weight_step)

        @pl.when(jnp.logical_or(slot == 2, jnp.logical_or(slot == 6, slot == 8)))
        def _():
            block(jnp.where(slot == 2, 0, jnp.where(slot == 6, 1, 7)))

        return carry

    lax.fori_loop(0, 12, gather_loop, 0)

    def last_hop_loop(h, carry):
        for way in range(2):
            a_pair(way, 2, h).wait_recv()
            a_copy(way, 3, way, h).start()

        @pl.when(h < 2)
        def _():
            block(2 + 4 * h)

        return carry

    lax.fori_loop(0, HEADS_HERE, last_hop_loop, 0)
    weight_wait()
    term = g_term(g_owner(0, 0))
    for h in range(HEADS_HERE):
        for way in range(2):
            g_fresh(way, 0, way, h, g_part(term, way, h))
    def third_hop_loop(n, carry):
        block(3 + 2 * n)
        return carry

    lax.fori_loop(0, 2, third_hop_loop, 0)
    for way in range(2):
        g_make_term(way, 1)
    for h in range(HEADS_HERE):
        for way in range(2):
            g_fresh(way, 1, 1 - way, h, gterm[1, way, 1 - way, h])
    for h in range(HEADS_HERE):
        for way in range(2):
            a_copy(way, 3, way, h).wait_recv()
    block(4)

    def reduce_loop(slot, carry):
        s, k = 1 + lax.div(slot + 3, 6), lax.rem(slot + 3, 6)
        h = jnp.where(slot < 3, slot, lax.div(k, 2))
        for way in range(2):
            image = jnp.where(slot < 3, way, lax.rem(k, 2))
            g_copy(way, s - 1, image, h).wait_recv()
            total = gterm[lax.rem(s, 2), way, image, h] + grecv[way, s - 1, image, h].astype(F32)
            g_fresh(way, s, image, h, total)

        @pl.when(slot == SCATTER_SLOTS[0])
        def _():
            for index in range(NZ):
                gw_copy(index, gw_owner(index)).wait_recv()

        at_slot(slot, tuple(enumerate(SCATTER_SLOTS)), scatter_step)
        for moment, way, step in ((1, 0, 2), (2, 1, 2), (5, 0, 3), (7, 1, 3), (11, 0, 4)):
            @pl.when(slot == moment)
            def _():
                g_make_term(way, step)

        for j in range(2):
            at_slot_of(slot, PART_SLOTS[j], lambda tile: output_part(tile, j))

        @pl.when(slot == SCATTER_SLOTS[4])
        def _():
            gw_result().start()
            for i, j in quarters:
                for n in range(3):
                    p1_copy(i, j, n).wait_send()
            for index in range(NZ):
                gw_copy(index, gw_owner(index)).wait_send()

        @pl.when(slot == 10)
        def _():
            weight_sent()

        @pl.when(slot == 12)
        def _():
            for way, s, image, h in gather_chunks:
                if s in (0, 3):
                    a_copy(way, s, image, h).wait_send()
                elif image == 0:
                    a_pair(way, s, h).wait_send()

        @pl.when(slot == 14)
        def _():
            for way, s, image, h in reduce_chunks:
                if s < 2:
                    g_copy(way, s, image, h).wait_send()

        return carry

    chunks = [(way, image, h) for way in range(2) for image in range(2) for h in range(HEADS_HERE)]
    gather_chunks = [(way, s, image, h) for s in range(4) for way, image, h in chunks if s < 3 or way == image]
    reduce_chunks = [(way, s, image, h) for s in range(4) for way, image, h in chunks if s > 0 or way == image]
    lax.fori_loop(0, 15, reduce_loop, 0)

    def backward_loop(h, carry):
        for image in range(2):
            total = gterm[0, 0, image, h]
            for way in range(2):
                g_copy(way, 3, image, h).wait_recv()
                total = total + grecv[way, 3, image, h].astype(F32)
            backward(image, h, total.astype(BF16))
        for copy in grad_copies(h):
            copy.start()

        @pl.when(h == 0)
        def _():
            for way, s, image, head in reduce_chunks:
                if s == 2:
                    g_copy(way, s, image, head).wait_send()

        @pl.when(h == 1)
        def _():
            for i, j in quarters:
                for n in range(3):
                    p2_copy(i, j, n).wait_send()
            for tile in range(4):
                output_copy(tile).wait()
            gw_result().wait()

        return carry

    lax.fori_loop(0, HEADS_HERE, backward_loop, 0)

    for way, s, image, h in reduce_chunks:
        if s == 3:
            g_copy(way, s, image, h).wait_send()
    for h in range(HEADS_HERE):
        for copy in grad_copies(h):
            copy.wait()


def store_kernel(*refs):
    made, results, held, load_sem, store_sem = refs[:5], refs[5:10], refs[10:15], refs[15], refs[16]
    parts = [(n, part) for n in range(5) for part in range(STORE_PARTS)]

    def piece(ref, part):
        rows = ref.shape[0] // STORE_PARTS
        return ref.at[pl.ds(part * rows, rows)]

    loads = [
        pltpu.make_async_copy(piece(made[n], part), piece(held[n], part), load_sem.at[n, part]) for n, part in parts
    ]
    stores = [
        pltpu.make_async_copy(piece(held[n], part), piece(results[n], part), store_sem.at[n, part])
        for n, part in parts
    ]
    for load in loads:
        load.start()
    for load, store in zip(loads, stores):
        load.wait()
        store.start()
    for store in stores:
        store.wait()


def per_device(queries, keys_in, values_in, query_gain, key_gain, out_weight, cotangent):
    dma = pltpu.SemaphoreType.DMA
    unit = (2, HEADS_HERE, PATCHES, HEAD_DIM)
    square = (2, HEADS_HERE, PATCHES, PATCHES)
    quarter = (HALF_ROWS, HALF_COLS)
    scratch = [pltpu.VMEM(a.shape, BF16) for a in (queries, keys_in, values_in, out_weight, cotangent)]
    scratch += [pltpu.VMEM((HEADS_HERE, 1, HEAD_DIM), F32)] * 2
    scratch += [pltpu.VMEM(a.shape, BF16) for a in (cotangent, queries, queries, queries, out_weight)]
    scratch += [
        pltpu.VMEM((2, NY, NX, 2, 2) + quarter, BF16),
        pltpu.VMEM((NZ * HEADS_HERE, 2 * PATCHES, HEAD_DIM), BF16),
        pltpu.VMEM(square, F32),
        pltpu.VMEM(square, BF16),
        pltpu.VMEM(unit, F32),
        pltpu.VMEM(unit, F32),
        pltpu.VMEM(unit, F32),
        pltpu.VMEM(unit, F32),
        pltpu.VMEM(unit, BF16),
        pltpu.VMEM(unit, BF16),
        pltpu.VMEM((2, 4) + unit, BF16),
        pltpu.VMEM((2, 4) + unit, BF16),
        pltpu.VMEM((2, 2) + unit, F32),
        pltpu.VMEM((2, NY, NX, 2, 2) + quarter, BF16),
        pltpu.VMEM((NY, NX, 2, 2) + quarter, BF16),
        pltpu.VMEM((2, 2, 3, 4) + quarter, BF16),
        pltpu.VMEM((2, 2, 3, 4) + quarter, BF16),
        pltpu.VMEM((2, 2, 3) + quarter, BF16),
        pltpu.VMEM((2, 2, 3) + quarter, BF16),
        pltpu.VMEM((2, 2, 4) + quarter, F32),
    ]
    ring4, ring8 = (2, 2, 3), (2, 4, 2, HEADS_HERE)
    scratch += [dma((5,)), dma((4,)), dma((3, HEADS_HERE)), dma]
    scratch += [dma(ring4), dma(ring4), dma(ring4), dma(ring4), dma, dma]
    scratch += [dma(ring4), dma(ring4), dma(ring4), dma(ring4)]
    scratch += [dma(ring8), dma(ring8), dma(ring8), dma(ring8), dma((NZ,)), dma((NZ,))]
    scratch += [dma(ring4), dma(ring4), dma(ring4), dma(ring4)]
    vmem = pl.BlockSpec(memory_space=pltpu.VMEM)
    anywhere = pl.BlockSpec(memory_space=pl.ANY)
    tokens, features = queries.shape
    results = [
        jax.ShapeDtypeStruct(cotangent.shape, BF16),
        jax.ShapeDtypeStruct((tokens, features), BF16),
        jax.ShapeDtypeStruct((tokens, features), BF16),
        jax.ShapeDtypeStruct((tokens, features), BF16),
        jax.ShapeDtypeStruct(out_weight.shape, BF16),
    ]
    made = pl.pallas_call(
        block_kernel,
        out_shape=results,
        in_specs=[anywhere] * 3 + [vmem] * 2 + [anywhere] * 2,
        out_specs=[anywhere] * 5,
        scratch_shapes=scratch,
        compiler_params=pltpu.CompilerParams(
            collective_id=0, has_side_effects=True, vmem_limit_bytes=60 * 1024 * 1024
        ),
        cost_estimate=pl.CostEstimate(flops=8_000_000_000, bytes_accessed=4_200_000, transcendentals=400_000),
    )(
        queries, keys_in, values_in, query_gain, key_gain, out_weight, cotangent
    )
    return pl.pallas_call(
        store_kernel,
        out_shape=results,
        in_specs=[anywhere] * 5,
        out_specs=[anywhere] * 5,
        scratch_shapes=[pltpu.VMEM(a.shape, a.dtype) for a in results] + [dma((5, STORE_PARTS))] * 2,
        compiler_params=pltpu.CompilerParams(vmem_limit_bytes=60 * 1024 * 1024),
    )(*made)


def solution(mesh):
    placed = (
        P("row", "col"),
        P("row", "col"),
        P("row", "col"),
        P("col"),
        P("col"),
        P("row", "col"),
        P("row", "col"),
    )
    return jax.shard_map(
        per_device,
        mesh=mesh,
        in_specs=placed,
        out_specs=(P("row", "col"),) * 5,
        check_vma=False,
    )
```

```python
import jax
import jax.numpy as jnp
from jax import lax
from jax.experimental import pallas as pl
from jax.experimental.pallas import tpu as pltpu
from jax.sharding import PartitionSpec as P

HEAD_DIM = 128
PATCHES = 256
HEADS_HERE = 3
NX, NY, NZ = 4, 4, 8
SHARD_ROWS = 96
HALF_ROWS = 48
HALF_COLS = 384
TILE_ROWS = 128
PART_SLOTS = ((1, 2, 3, 5), (6, 7, 8, 10))
SCATTER_SLOTS = (0, 4, 9, 11, 13)
STORE_PARTS = 2
EPSILON = 1e-06
MESH = pl.DeviceIdType.MESH
BF16 = jnp.bfloat16
F32 = jnp.float32


def dot_nn(a, b):
    return jnp.dot(a, b, preferred_element_type=F32)


def dot_nt(a, b):
    return lax.dot_general(a, b, (((1,), (1,)), ((), ())), preferred_element_type=F32)


def dot_tn(a, b):
    return lax.dot_general(a, b, (((0,), (0,)), ((), ())), preferred_element_type=F32)


def block_kernel(
    q_in, k_in, v_in, qg_in, kg_in, w_in, ct_in,
    out_hbm, gq_hbm, gk_hbm, gv_hbm, gw_hbm,
    q_ref, k_ref, v_ref, w_ref, ct_ref, qg_ref, kg_ref,
    out_ref, gq_ref, gk_ref, gv_ref, gw_ref,
    wall, aall, prob, plow, qhat, khat, qrs, krs, qn, kn,
    gsend, grecv, gterm, gwb, sib, s1, r1, s2, r2, c1,
    load_sem, out_sem, grad_sem, gw_sem,
    w1_send, w1_recv, w2_send, w2_recv, ws0_send, ws0_recv, ws1_send, ws1_recv, ws2_send, ws2_recv,
    a_send, a_recv, g_send, g_recv, sib_send, sib_recv, p1_send, p1_recv, p2_send, p2_recv,
):
    row = lax.axis_index("row")
    z = lax.axis_index("col")
    core = lax.rem(row, 2)
    x = lax.rem(lax.div(row, 2), NX)
    y = lax.div(row, 2 * NX)
    scale = HEAD_DIM ** (-0.5)

    def device(yy, xx, cc, zz):
        return ((yy * NX + xx) * 2 + cc, zz)

    def x_turn(j):
        return device(y, lax.rem(x + 1 + 2 * j, NX), core, z)

    def y_turn(j):
        return device(lax.rem(y + 1 + 2 * j, NY), x, core, z)

    def z_turn(way):
        return (row, lax.rem(z + 1 + 6 * way, NZ))

    sibling = device(y, x, 1 - core, z)

    barrier = pltpu.get_barrier_semaphore()
    for peer in (x_turn(0), x_turn(1), y_turn(0), y_turn(1), z_turn(0), z_turn(1), sibling):
        pl.semaphore_signal(barrier, inc=1, device_id=peer, device_id_type=MESH)

    loads = [
        pltpu.make_async_copy(source, target, load_sem.at[n])
        for n, (source, target) in enumerate(
            ((q_in, q_ref), (k_in, k_ref), (v_in, v_ref), (w_in, w_ref), (ct_in, ct_ref))
        )
    ]
    for load in loads:
        load.start()
    for h in range(HEADS_HERE):
        qg_ref[h, 0] = qg_in[h * HEAD_DIM : (h + 1) * HEAD_DIM]
        kg_ref[h, 0] = kg_in[h * HEAD_DIM : (h + 1) * HEAD_DIM]

    def remote(src, dst, send, recv, peer):
        return pltpu.make_async_remote_copy(
            src_ref=src, dst_ref=dst, send_sem=send, recv_sem=recv, device_id=peer, device_id_type=MESH
        )

    def behind(pos, steps, j):
        return lax.rem(pos + (4 - steps if j == 0 else steps), 4)

    def w1_ref(i, j, steps):
        if i == 0:
            return wall.at[j, y, behind(x, steps, j), core, i]
        return wall.at[j, behind(y, steps, j), x, core, i]

    def w2_ref(i, j, steps):
        if i == 0:
            return wall.at[j, behind(y, steps, j), :, core, i]
        return wall.at[j, :, behind(x, steps, j), core, i]

    def w1_copy(i, j, s):
        ref = w1_ref(i, j, s)
        return remote(ref, ref, w1_send.at[i, j, s], w1_recv.at[i, j, s], x_turn(j) if i == 0 else y_turn(j))

    def w2_copy(i, j, s):
        ref = w2_ref(i, j, s)
        return remote(ref, ref, w2_send.at[i, j, s], w2_recv.at[i, j, s], y_turn(j) if i == 0 else x_turn(j))

    def ws0_copy():
        ref = wall.at[:, y, x, core]
        return remote(ref, ref, ws0_send, ws0_recv, sibling)

    def ws1_copy(i, j, s):
        ref = w1_ref(i, j, s + 1)
        return remote(ref, ref, ws1_send.at[i, j, s], ws1_recv.at[i, j, s], sibling)

    def ws2_copy(i, j, s):
        ref = w2_ref(i, j, s + 1)
        return remote(ref, ref, ws2_send.at[i, j, s], ws2_recv.at[i, j, s], sibling)

    quarters = [(i, j) for i in range(2) for j in range(2)]

    def weight_step(t):
        for i, j in quarters:
            if t < 3:
                w1_copy(i, j, t).wait_recv()
                if t < 2:
                    w1_copy(i, j, t + 1).start()
                else:
                    w2_copy(i, j, 0).start()
                ws1_copy(i, j, t).start()
            else:
                w2_copy(i, j, t - 3).wait_recv()
                if t < 5:
                    w2_copy(i, j, t - 2).start()
                ws2_copy(i, j, t - 3).start()

    def weight_wait():
        ws0_copy().wait_recv()
        for i, j in quarters:
            for s in range(3):
                ws1_copy(i, j, s).wait_recv()
                ws2_copy(i, j, s).wait_recv()

    def weight_sent():
        ws0_copy().wait_send()
        for i, j in quarters:
            for s in range(3):
                w1_copy(i, j, s).wait_send()
                w2_copy(i, j, s).wait_send()
                ws1_copy(i, j, s).wait_send()
                ws2_copy(i, j, s).wait_send()

    def image_rows(image):
        return pl.ds(pl.multiple_of(image * PATCHES, PATCHES), PATCHES)

    def a_copy(way, s, image, h):
        origin = lax.rem(z + (NZ - s if way == 0 else s), NZ)
        ref = aall.at[origin * HEADS_HERE + h, image_rows(image)]
        return remote(ref, ref, a_send.at[way, s, image, h], a_recv.at[way, s, image, h], z_turn(way))

    def a_own(image, h):
        for way in range(2):
            a_copy(way, 0, image, h).start()

    def a_pair(way, s, h):
        origin = lax.rem(z + (NZ - s if way == 0 else s), NZ)
        ref = aall.at[origin * HEADS_HERE + h]
        return remote(ref, ref, a_send.at[way, s, 0, h], a_recv.at[way, s, 0, h], z_turn(way))

    def head_slice(image, h):
        return (pl.ds(image * PATCHES, PATCHES), pl.ds(pl.multiple_of(h * HEAD_DIM, HEAD_DIM), HEAD_DIM))

    def norm_forward(image, h, source, gain, hat, spread_ref, normed):
        inside = source[head_slice(image, h)].astype(F32)
        centred = inside - jnp.mean(inside, axis=-1, keepdims=True)
        spread = jnp.mean(centred * centred, axis=-1, keepdims=True)
        factor = lax.rsqrt(spread + EPSILON)
        unit = centred * factor
        hat[image, h] = unit
        spread_ref[image, h] = jnp.broadcast_to(factor, unit.shape)
        value = (unit * gain[h]).astype(BF16)
        normed[image, h] = value
        return value

    def forward(image, h):
        q_norm = norm_forward(image, h, q_ref, qg_ref, qhat, qrs, qn)
        k_norm = norm_forward(image, h, k_ref, kg_ref, khat, krs, kn)
        weights = jnp.exp(dot_nt(q_norm, k_norm) * scale)
        probabilities = weights * (1.0 / jnp.sum(weights, axis=-1, keepdims=True))
        low = probabilities.astype(BF16)
        prob[image, h] = probabilities
        plow[image, h] = low
        attended = dot_nn(low, v_ref[head_slice(image, h)]).astype(BF16)
        aall[z * HEADS_HERE + h, pl.ds(image * PATCHES, PATCHES)] = attended

    def norm_backward(grad, image, h, gain, hat, spread_ref):
        scaled = grad * gain[h]
        unit = hat[image, h]
        first = jnp.mean(scaled, axis=-1, keepdims=True)
        second = jnp.mean(scaled * unit, axis=-1, keepdims=True)
        return (spread_ref[image, h] * (scaled - first - unit * second)).astype(BF16)

    def backward(image, h, grad_attended):
        place = head_slice(image, h)
        probabilities = prob[image, h]
        gv_ref[place] = dot_tn(plow[image, h], grad_attended).astype(BF16)
        grad_probs = dot_nt(grad_attended, v_ref[place])
        inner = jnp.sum(probabilities * grad_probs, axis=-1, keepdims=True)
        grad_scores = (probabilities * (grad_probs - inner) * scale).astype(BF16)
        grad_q = dot_nn(grad_scores, kn[image, h])
        grad_k = dot_tn(grad_scores, qn[image, h])
        gq_ref[place] = norm_backward(grad_q, image, h, qg_ref, qhat, qrs)
        gk_ref[place] = norm_backward(grad_k, image, h, kg_ref, khat, krs)

    def weight_rows(j, o):
        piece = wall[j, lax.div(o, 2), pl.ds(2 * lax.rem(o, 2), 2)]
        return piece.reshape(HEADS_HERE * HEAD_DIM, HALF_COLS)

    def g_copy(way, s, image, h):
        at = (way, s, image, h)
        return remote(gsend.at[at], grecv.at[at], g_send.at[at], g_recv.at[at], z_turn(way))

    def g_term(owner):
        return dot_nt(ct_ref[:, :HALF_COLS], weight_rows(0, owner)) + dot_nt(
            ct_ref[:, HALF_COLS:], weight_rows(1, owner)
        )

    def g_part(term, image, h):
        return term[image * PATCHES : (image + 1) * PATCHES, h * HEAD_DIM : (h + 1) * HEAD_DIM]

    def g_owner(way, s):
        return lax.rem(z + (NZ + 4 - s if way == 0 else 4 + s), NZ)

    def g_make_term(way, s):
        term = g_term(g_owner(way, s))
        for image in range(2):
            for h in range(HEADS_HERE):
                gterm[s % 2, way, image, h] = g_part(term, image, h)

    def g_fresh(way, s, image, h, value):
        gsend[way, s, image, h] = value.astype(BF16)
        g_copy(way, s, image, h).start()

    def gw_copy(index, o):
        place = pl.ds(2 * lax.rem(o, 2), 2)
        return remote(
            gwb.at[1 - core, lax.div(o, 2), place],
            sib.at[lax.div(o, 2), place],
            sib_send.at[index],
            sib_recv.at[index],
            sibling,
        )

    def gw_block(index, o):
        panel = jnp.concatenate([aall[o * HEADS_HERE + h] for h in range(HEADS_HERE)], axis=1)
        product = dot_tn(panel, ct_ref[...]).astype(BF16)
        for j in range(2):
            value = product[:, j * HALF_COLS : (j + 1) * HALF_COLS]
            for xx in range(2):
                for cc in range(2):
                    for i in range(2):
                        at = (xx * 4 + cc * 2 + i) * HALF_ROWS
                        gwb[cc, lax.div(o, 2), 2 * lax.rem(o, 2) + xx, i, j] = value[at : at + HALF_ROWS]
        gw_copy(index, o).start()

    def gw_owner(index):
        return lax.rem(z + index, NZ)

    def chip_sum(i, j, d):
        if i == 0:
            return gwb[core, :, d, i, j].astype(F32) + sib[:, d, i, j].astype(F32)
        return gwb[core, d, :, i, j].astype(F32) + sib[d, :, i, j].astype(F32)

    def p1_copy(i, j, n):
        turn = 1 - j if n == 1 else j
        peer = x_turn(turn) if i == 0 else y_turn(turn)
        return remote(s1.at[i, j, n], r1.at[i, j, n], p1_send.at[i, j, n], p1_recv.at[i, j, n], peer)

    def p2_copy(i, j, n):
        turn = 1 - j if n == 1 else j
        peer = y_turn(turn) if i == 0 else x_turn(turn)
        return remote(s2.at[i, j, n], r2.at[i, j, n], p2_send.at[i, j, n], p2_recv.at[i, j, n], peer)

    def scatter_step(t):
        if t == 0:
            for n in range(2):
                for i, j in quarters:
                    s1[i, j, n] = chip_sum(i, j, behind(x if i == 0 else y, 2 - n, j)).astype(BF16)
                    p1_copy(i, j, n).start()
            return
        for i, j in quarters:
            first, second = (x, y) if i == 0 else (y, x)
            if t == 1:
                p1_copy(i, j, 0).wait_recv()
                total = chip_sum(i, j, behind(first, 3, j)) + r1[i, j, 0].astype(F32)
                s1[i, j, 2] = total.astype(BF16)
                p1_copy(i, j, 2).start()
            elif t == 2:
                total = chip_sum(i, j, first)
                for n in (1, 2):
                    p1_copy(i, j, n).wait_recv()
                    total = total + r1[i, j, n].astype(F32)
                c1[i, j] = total
                for n in range(2):
                    s2[i, j, n] = c1[i, j, behind(second, 2 - n, j)].astype(BF16)
                    p2_copy(i, j, n).start()
            elif t == 3:
                p2_copy(i, j, 0).wait_recv()
                total = c1[i, j, behind(second, 3, j)] + r2[i, j, 0].astype(F32)
                s2[i, j, 2] = total.astype(BF16)
                p2_copy(i, j, 2).start()
            else:
                total = c1[i, j, second]
                for n in (1, 2):
                    p2_copy(i, j, n).wait_recv()
                    total = total + r2[i, j, n].astype(F32)
                gw_ref[
                    i * HALF_ROWS : (i + 1) * HALF_ROWS, j * HALF_COLS : (j + 1) * HALF_COLS
                ] = total.astype(BF16)

    def output_copy(tile):
        rows = pl.ds(pl.multiple_of(tile * TILE_ROWS, TILE_ROWS), TILE_ROWS)
        return pltpu.make_async_copy(out_ref.at[rows], out_hbm.at[rows], out_sem.at[tile])

    def output_part(tile, j):
        rows = pl.ds(pl.multiple_of(tile * TILE_ROWS, TILE_ROWS), TILE_ROWS)
        total = None
        for o in range(NZ):
            panel = jnp.concatenate([aall[o * HEADS_HERE + h, rows] for h in range(HEADS_HERE)], axis=1)
            term = dot_nn(panel, weight_rows(j, o))
            total = term if total is None else total + term
        out_ref[rows, j * HALF_COLS : (j + 1) * HALF_COLS] = total.astype(BF16)
        if j == 1:
            output_copy(tile).start()

    def grad_copies(h):
        columns = pl.ds(pl.multiple_of(h * HEAD_DIM, HEAD_DIM), HEAD_DIM)
        return [
            pltpu.make_async_copy(source.at[:, columns], target.at[:, columns], grad_sem.at[n, h])
            for n, (source, target) in enumerate(((gq_ref, gq_hbm), (gk_ref, gk_hbm), (gv_ref, gv_hbm)))
        ]

    def gw_result():
        return pltpu.make_async_copy(gw_ref, gw_hbm, gw_sem)

    for load in loads[:3]:
        load.wait()
    forward(0, 0)
    pl.semaphore_wait(barrier, 7)
    a_own(0, 0)
    loads[3].wait()
    for i, j in quarters:
        wall[j, y, x, core, i] = w_ref[
            i * HALF_ROWS : (i + 1) * HALF_ROWS, j * HALF_COLS : (j + 1) * HALF_COLS
        ]
    for i, j in quarters:
        w1_copy(i, j, 0).start()
    ws0_copy().start()
    forward(1, 0)
    a_own(1, 0)

    def at_slot(slot, moments, action):
        for t, moment in moments:
            @pl.when(slot == moment)
            def _():
                action(t)

    def at_slot_of(slot, moments, action):
        hit, tile = slot == moments[0], jnp.where(slot == moments[0], 0, 0)
        for n, moment in enumerate(moments[1:]):
            hit, tile = jnp.logical_or(hit, slot == moment), jnp.where(slot == moment, n + 1, tile)

        @pl.when(hit)
        def _():
            action(tile)

    def forward_loop(h, carry):
        for image in range(2):
            forward(image, h)
        for way in range(2):
            a_pair(way, 0, h).start()
        at_slot(h, ((0, 1), (1, 2)), weight_step)
        return carry

    lax.fori_loop(1, HEADS_HERE, forward_loop, 0)
    loads[4].wait()

    def block(index):
        gw_block(index, gw_owner(index))

    def gather_loop(slot, carry):
        k = lax.rem(slot, 6)
        for s in (1, 2):
            @pl.when(lax.div(slot, 6) == s - 1)
            def _():
                @pl.when(lax.rem(k, 2) == 0)
                def _():
                    h = lax.div(k, 2)
                    for way in range(2):
                        if s == 1:
                            @pl.when(h == 0)
                            def _():
                                for image in range(2):
                                    a_copy(way, 0, image, 0).wait_recv()

                            @pl.when(h > 0)
                            def _():
                                a_pair(way, 0, h).wait_recv()
                        else:
                            a_pair(way, 1, h).wait_recv()
                        a_pair(way, s, h).start()

        at_slot(slot, ((2, 1), (3, 4), (4, 7), (5, 10)), weight_step)

        @pl.when(jnp.logical_or(slot == 2, jnp.logical_or(slot == 6, slot == 8)))
        def _():
            block(jnp.where(slot == 2, 0, jnp.where(slot == 6, 1, 7)))

        return carry

    lax.fori_loop(0, 12, gather_loop, 0)

    def last_hop_loop(h, carry):
        for way in range(2):
            a_pair(way, 2, h).wait_recv()
            a_copy(way, 3, way, h).start()

        @pl.when(h < 2)
        def _():
            block(2 + 4 * h)

        return carry

    lax.fori_loop(0, HEADS_HERE, last_hop_loop, 0)
    weight_wait()
    term = g_term(g_owner(0, 0))
    for h in range(HEADS_HERE):
        for way in range(2):
            g_fresh(way, 0, way, h, g_part(term, way, h))
    def third_hop_loop(n, carry):
        block(3 + 2 * n)
        return carry

    lax.fori_loop(0, 2, third_hop_loop, 0)
    for way in range(2):
        g_make_term(way, 1)
    for h in range(HEADS_HERE):
        for way in range(2):
            g_fresh(way, 1, 1 - way, h, gterm[1, way, 1 - way, h])
    for h in range(HEADS_HERE):
        for way in range(2):
            a_copy(way, 3, way, h).wait_recv()
    block(4)

    def reduce_loop(slot, carry):
        s, k = 1 + lax.div(slot + 3, 6), lax.rem(slot + 3, 6)
        h = jnp.where(slot < 3, slot, lax.div(k, 2))
        for way in range(2):
            image = jnp.where(slot < 3, way, lax.rem(k, 2))
            g_copy(way, s - 1, image, h).wait_recv()
            total = gterm[lax.rem(s, 2), way, image, h] + grecv[way, s - 1, image, h].astype(F32)
            g_fresh(way, s, image, h, total)

        @pl.when(slot == SCATTER_SLOTS[0])
        def _():
            for index in range(NZ):
                gw_copy(index, gw_owner(index)).wait_recv()

        at_slot(slot, tuple(enumerate(SCATTER_SLOTS)), scatter_step)
        for moment, way, step in ((1, 0, 2), (2, 1, 2), (5, 0, 3), (7, 1, 3), (11, 0, 4)):
            @pl.when(slot == moment)
            def _():
                g_make_term(way, step)

        for j in range(2):
            at_slot_of(slot, PART_SLOTS[j], lambda tile: output_part(tile, j))

        @pl.when(slot == SCATTER_SLOTS[4])
        def _():
            gw_result().start()
            for i, j in quarters:
                for n in range(3):
                    p1_copy(i, j, n).wait_send()
            for index in range(NZ):
                gw_copy(index, gw_owner(index)).wait_send()

        @pl.when(slot == 10)
        def _():
            weight_sent()

        @pl.when(slot == 12)
        def _():
            for way, s, image, h in gather_chunks:
                if s == 3 or (s == 0 and h == 0):
                    a_copy(way, s, image, h).wait_send()
                elif image == 0:
                    a_pair(way, s, h).wait_send()

        @pl.when(slot == 14)
        def _():
            for way, s, image, h in reduce_chunks:
                if s < 2:
                    g_copy(way, s, image, h).wait_send()

        return carry

    chunks = [(way, image, h) for way in range(2) for image in range(2) for h in range(HEADS_HERE)]
    gather_chunks = [(way, s, image, h) for s in range(4) for way, image, h in chunks if s < 3 or way == image]
    reduce_chunks = [(way, s, image, h) for s in range(4) for way, image, h in chunks if s > 0 or way == image]
    lax.fori_loop(0, 15, reduce_loop, 0)

    def backward_loop(h, carry):
        for image in range(2):
            total = gterm[0, 0, image, h]
            for way in range(2):
                g_copy(way, 3, image, h).wait_recv()
                total = total + grecv[way, 3, image, h].astype(F32)
            backward(image, h, total.astype(BF16))
        for copy in grad_copies(h):
            copy.start()

        @pl.when(h == 0)
        def _():
            for way, s, image, head in reduce_chunks:
                if s == 2:
                    g_copy(way, s, image, head).wait_send()

        @pl.when(h == 1)
        def _():
            for i, j in quarters:
                for n in range(3):
                    p2_copy(i, j, n).wait_send()
            for tile in range(4):
                output_copy(tile).wait()
            gw_result().wait()

        return carry

    lax.fori_loop(0, HEADS_HERE, backward_loop, 0)

    for way, s, image, h in reduce_chunks:
        if s == 3:
            g_copy(way, s, image, h).wait_send()
    for h in range(HEADS_HERE):
        for copy in grad_copies(h):
            copy.wait()


def store_kernel(*refs):
    made, results, held, load_sem, store_sem = refs[:5], refs[5:10], refs[10:15], refs[15], refs[16]
    parts = [(n, part) for n in range(5) for part in range(STORE_PARTS)]

    def piece(ref, part):
        rows = ref.shape[0] // STORE_PARTS
        return ref.at[pl.ds(part * rows, rows)]

    loads = [
        pltpu.make_async_copy(piece(made[n], part), piece(held[n], part), load_sem.at[n, part]) for n, part in parts
    ]
    stores = [
        pltpu.make_async_copy(piece(held[n], part), piece(results[n], part), store_sem.at[n, part])
        for n, part in parts
    ]
    for load in loads:
        load.start()
    for load, store in zip(loads, stores):
        load.wait()
        store.start()
    for store in stores:
        store.wait()


def per_device(queries, keys_in, values_in, query_gain, key_gain, out_weight, cotangent):
    dma = pltpu.SemaphoreType.DMA
    unit = (2, HEADS_HERE, PATCHES, HEAD_DIM)
    square = (2, HEADS_HERE, PATCHES, PATCHES)
    quarter = (HALF_ROWS, HALF_COLS)
    scratch = [pltpu.VMEM(a.shape, BF16) for a in (queries, keys_in, values_in, out_weight, cotangent)]
    scratch += [pltpu.VMEM((HEADS_HERE, 1, HEAD_DIM), F32)] * 2
    scratch += [pltpu.VMEM(a.shape, BF16) for a in (cotangent, queries, queries, queries, out_weight)]
    scratch += [
        pltpu.VMEM((2, NY, NX, 2, 2) + quarter, BF16),
        pltpu.VMEM((NZ * HEADS_HERE, 2 * PATCHES, HEAD_DIM), BF16),
        pltpu.VMEM(square, F32),
        pltpu.VMEM(square, BF16),
        pltpu.VMEM(unit, F32),
        pltpu.VMEM(unit, F32),
        pltpu.VMEM(unit, F32),
        pltpu.VMEM(unit, F32),
        pltpu.VMEM(unit, BF16),
        pltpu.VMEM(unit, BF16),
        pltpu.VMEM((2, 4) + unit, BF16),
        pltpu.VMEM((2, 4) + unit, BF16),
        pltpu.VMEM((2, 2) + unit, F32),
        pltpu.VMEM((2, NY, NX, 2, 2) + quarter, BF16),
        pltpu.VMEM((NY, NX, 2, 2) + quarter, BF16),
        pltpu.VMEM((2, 2, 3, 4) + quarter, BF16),
        pltpu.VMEM((2, 2, 3, 4) + quarter, BF16),
        pltpu.VMEM((2, 2, 3) + quarter, BF16),
        pltpu.VMEM((2, 2, 3) + quarter, BF16),
        pltpu.VMEM((2, 2, 4) + quarter, F32),
    ]
    ring4, ring8 = (2, 2, 3), (2, 4, 2, HEADS_HERE)
    scratch += [dma((5,)), dma((4,)), dma((3, HEADS_HERE)), dma]
    scratch += [dma(ring4), dma(ring4), dma(ring4), dma(ring4), dma, dma]
    scratch += [dma(ring4), dma(ring4), dma(ring4), dma(ring4)]
    scratch += [dma(ring8), dma(ring8), dma(ring8), dma(ring8), dma((NZ,)), dma((NZ,))]
    scratch += [dma(ring4), dma(ring4), dma(ring4), dma(ring4)]
    vmem = pl.BlockSpec(memory_space=pltpu.VMEM)
    anywhere = pl.BlockSpec(memory_space=pl.ANY)
    tokens, features = queries.shape
    results = [
        jax.ShapeDtypeStruct(cotangent.shape, BF16),
        jax.ShapeDtypeStruct((tokens, features), BF16),
        jax.ShapeDtypeStruct((tokens, features), BF16),
        jax.ShapeDtypeStruct((tokens, features), BF16),
        jax.ShapeDtypeStruct(out_weight.shape, BF16),
    ]
    made = pl.pallas_call(
        block_kernel,
        out_shape=results,
        in_specs=[anywhere] * 3 + [vmem] * 2 + [anywhere] * 2,
        out_specs=[anywhere] * 5,
        scratch_shapes=scratch,
        compiler_params=pltpu.CompilerParams(
            collective_id=0, has_side_effects=True, vmem_limit_bytes=60 * 1024 * 1024
        ),
        cost_estimate=pl.CostEstimate(flops=8_000_000_000, bytes_accessed=4_200_000, transcendentals=400_000),
    )(
        queries, keys_in, values_in, query_gain, key_gain, out_weight, cotangent
    )
    return pl.pallas_call(
        store_kernel,
        out_shape=results,
        in_specs=[anywhere] * 5,
        out_specs=[anywhere] * 5,
        scratch_shapes=[pltpu.VMEM(a.shape, a.dtype) for a in results] + [dma((5, STORE_PARTS))] * 2,
        compiler_params=pltpu.CompilerParams(vmem_limit_bytes=60 * 1024 * 1024),
    )(*made)


def solution(mesh):
    placed = (
        P("row", "col"),
        P("row", "col"),
        P("row", "col"),
        P("col"),
        P("col"),
        P("row", "col"),
        P("row", "col"),
    )
    return jax.shard_map(
        per_device,
        mesh=mesh,
        in_specs=placed,
        out_specs=(P("row", "col"),) * 5,
        check_vma=False,
    )
```
